128 devices in a mesh: tm: 8 (over x_hi, y), space: 16 (over z, x_lo, core).
Axes of the slice: x: 4 (x_hi: 2, x_lo: 2; x = x_hi * 2 + x_lo), y: 4, z: 4, core: 2. Of those that a mesh axis runs over, the one named last changes fastest.
Arguments:
- forcing: float32 [8, 128, 16384], P('tm', 'space'), may hold values from -6 to 6
- conductivity: float32 [128, 16384], P('space'), may hold values from 0.1 to 1
Outputs:
- solution: float32 [8, 128, 16384], P('tm', 'space')
The draws below stay inside these ranges and needn't reach their ends.
All inputs are finite; a program needn't handle non-finite values.
Results may differ from the reference program's by a relative error of at most 0.0001.
Values sent between devices are 32-bit elements; how exact they have to be, the bound alone decides.
No kernel may reach another device: no remote copies, remote signals or barrier semaphores. Data moves between devices by JAX's collectives and lax.ppermute only.
A program may use at most 64 MiB of HBM per device.

```python
import math
import jax
import jax.numpy as jnp

NY = 16384
ITERS = 3
NT = 8
NX = 128


def block_scale(stream_key, dims, shards, low, high):
    gain = 1.0
    for axis_at, blocks in shards:
        steps = jax.random.uniform(jax.random.fold_in(jax.random.fold_in(stream_key, 6), axis_at), (blocks,), jnp.float32, low / len(shards), high / len(shards))
        gain = gain * jnp.repeat(jnp.exp(steps), dims[axis_at] // blocks).reshape((-1,) + (1,) * (len(dims) - 1 - axis_at))
    return gain


def centred(key, dims, spread, most, split=(), kind=jnp.bfloat16):
    factor_of = block_scale(key, dims, split, -0.22, 0.18) if split else 1.0
    drawn = jax.random.normal(key, dims, jnp.float32) * spread * factor_of
    return jnp.minimum(jnp.maximum(drawn, -most), most).astype(kind)


def setup_inputs(seed: int = 0) -> dict:
    key_list = jax.random.split(jax.random.key(seed), 3)
    return {
        "forcing": centred(key_list[0], (NT, NX, NY), 1.0, 6.0, ((0, 8), (1, 16)), jnp.float32),
        "conductivity": jnp.clip(jnp.exp(math.log(1.0) - 2.3025851 * jax.random.uniform(key_list[1], (NX, NY), jnp.float32) ** block_scale(key_list[1], (NX, NY), ((0, 16),), -0.2, 0.2)), 0.1, 1.0),
    }


def edge_weights(kpad):
    center = kpad[1:-1, 1:-1]
    north = 0.5 * (center + kpad[:-2, 1:-1])
    south = 0.5 * (center + kpad[2:, 1:-1])
    west = 0.5 * (center + kpad[1:-1, :-2])
    east = 0.5 * (center + kpad[1:-1, 2:])
    diag = 1.0 + north + south + west + east
    return (north, south, west, east, diag)

def neighbours(field, north, south, west, east):
    padded = jnp.pad(field, ((0, 0), (1, 1), (1, 1)))
    total = north * padded[:, :-2, 1:-1] + south * padded[:, 2:, 1:-1]
    return total + west * padded[:, 1:-1, :-2] + east * padded[:, 1:-1, 2:]

def operate(field, weights):
    north, south, west, east, diag = weights
    stepped = diag * field - neighbours(field, north, south, west, east)
    earlier = jnp.concatenate([jnp.zeros_like(field[:1]), field[:-1]], 0)
    return jnp.flip(stepped - earlier, 0)

def precondition(field, weights, scale):
    north, south, west, east, diag = weights

    def apply_g(term):
        return scale * neighbours(scale * term, north, south, west, east)
    first = scale * field
    second = apply_g(first)
    third = 2.0 * apply_g(second) - first
    fourth = 2.0 * apply_g(third) - second
    return scale * (first + 0.5 * second + 0.25 * third + 0.125 * fourth)

def reference(forcing, conductivity):
    weights = edge_weights(jnp.pad(conductivity, 1))
    scale = 1.0 / jnp.sqrt(weights[4])
    vec = jnp.flip(forcing, 0)
    vec_old = jnp.zeros_like(vec)
    zvec = precondition(vec, weights, scale)
    gamma = jnp.sqrt(jnp.sum(zvec * vec))
    gamma_old = jnp.float32(1.0)
    wvec = jnp.zeros_like(vec)
    wvec_old = jnp.zeros_like(vec)
    solution = jnp.zeros_like(vec)
    cos_now = jnp.float32(1.0)
    cos_old = jnp.float32(1.0)
    sin_now = jnp.float32(0.0)
    sin_old = jnp.float32(0.0)
    eta = gamma
    for step in range(ITERS):
        zvec = zvec / gamma
        image = operate(zvec, weights)
        delta = jnp.sum(image * zvec)
        vec_new = image - delta / gamma * vec - gamma / gamma_old * vec_old
        zvec_new = precondition(vec_new, weights, scale)
        gamma_new = jnp.sqrt(jnp.sum(zvec_new * vec_new))
        alpha_zero = cos_now * delta - cos_old * sin_now * gamma
        alpha_one = jnp.sqrt(alpha_zero * alpha_zero + gamma_new * gamma_new)
        alpha_two = sin_now * delta + cos_old * cos_now * gamma
        alpha_three = sin_old * gamma
        cos_new = alpha_zero / alpha_one
        sin_new = gamma_new / alpha_one
        wvec_new = (zvec - alpha_three * wvec_old - alpha_two * wvec) / alpha_one
        solution = solution + cos_new * eta * wvec_new
        eta = -sin_new * eta
        vec_old, vec, zvec = (vec, vec_new, zvec_new)
        gamma_old, gamma = (gamma, gamma_new)
        wvec_old, wvec = (wvec, wvec_new)
        cos_old, cos_now, sin_old, sin_now = (cos_now, cos_new, sin_now, sin_new)
    return solution
```

```python
import jax
import jax.numpy as jnp
from jax import lax
from jax.experimental import pallas as pl
from jax.experimental.pallas import tpu as pltpu
from jax.sharding import PartitionSpec as P

STEPS = 8
STRIPS = 16
BLOCKS = STEPS * STRIPS
LANES = 128
HALO = 16
WIDE = LANES + 2 * HALO
PAD = 8
TALL = WIDE + 2 * PAD
TILES = WIDE // 8
SEND = 12
BACK = 25


def lane_of(shape):
    return lax.broadcasted_iota(jnp.int32, shape, 1)


def row_of(shape):
    return lax.broadcasted_iota(jnp.int32, shape, 0)


def pack_kernel(step_ref, f_ref, k_ref, out_ref):
    step = step_ref[0]
    shift = lax.rem(jnp.int32(48) - 32 * step + 256, jnp.int32(128))
    lane = lane_of((8, LANES))
    zero = jnp.zeros((8, LANES), jnp.float32)

    def tile(ref, d):
        return ref[:, d * LANES : (d + 1) * LANES]

    def rolled(d):
        if d < 0 or d >= BLOCKS:
            return zero, zero
        return pltpu.roll(tile(f_ref, d), 16, 1), pltpu.roll(tile(k_ref, d), shift, 1)

    first, last = step == 0, step == 4
    before, here = rolled(-1), rolled(0)
    for d in range(BLOCKS):
        after = rolled(d + 1)
        lower = jnp.where(first, before[1], here[1])
        upper = jnp.where(last, after[1], here[1])
        side = jnp.where(lane < 16, before[0], jnp.where(lane < 32, after[0], jnp.where(lane < 48, lower, upper)))
        folded = jnp.where(lane < 64, side, pltpu.roll(pltpu.roll(side, 64, 1), 4, 0))
        out_ref[d * SEND : d * SEND + 8, :] = tile(f_ref, d)
        out_ref[d * SEND + 8 : d * SEND + 12, :] = folded[:4]
        before, here = here, after


def main_kernel(block_ref, in_ref, out_ref, sides, k, s, gn, gw, r0, r1, a, b, q0, q1, q2):
    lane = lane_of((8, LANES))
    sub = row_of((8, LANES))
    edge = jnp.zeros((PAD, LANES), jnp.float32)
    for ref in (k, s, gn, gw):
        ref[0:PAD, :] = edge
        ref[PAD + WIDE : TALL, :] = edge
    for ref in (r0, r1, a, b, q0, q1, q2):
        for t in range(STEPS):
            ref[t, 0:PAD, :] = edge
            ref[t, PAD + WIDE : TALL, :] = edge

    for t in range(STEPS):
        rows = []
        for i in range(STRIPS):
            at = SEND * (STRIPS * t + i)
            rows.append(in_ref[at : at + 8, :])
            piece = in_ref[at + 8 : at + 12, :]
            sides[8 * i : 8 * i + 4, :] = piece
            sides[8 * i + 4 : 8 * i + 8, :] = pltpu.roll(piece, 64, 1)
        r0[t, PAD + HALO : PAD + HALO + LANES, :] = jnp.concatenate(rows, 0).T
        turned = sides[...].T
        r0[t, PAD : PAD + HALO, :] = turned[0:16]
        r0[t, PAD + HALO + LANES : PAD + WIDE, :] = turned[16:32]
        if t < 5:
            k[PAD + 32 * t : PAD + 32 * t + 32, :] = turned[32:64]

    def at(i, offset=0):
        return pl.ds(pl.multiple_of(8 * i + PAD, 8) + offset, 8)

    def halves(i):
        mid = k[at(i), :]
        up = jnp.where(lane == 0, 0.0, pltpu.roll(mid, 1, 1))
        return mid, 0.5 * (mid + up), 0.5 * (mid + k[at(i, -1), :])

    @pl.loop(0, TILES)
    def _(i):
        mid, north, west = halves(i)
        down = jnp.where(lane == LANES - 1, 0.0, pltpu.roll(mid, LANES - 1, 1))
        south = 0.5 * (mid + down)
        east = 0.5 * (mid + k[at(i, 1), :])
        scale = 1.0 / jnp.sqrt(1.0 + north + south + west + east)
        s[at(i), :] = scale
        for t in range(STEPS):
            r0[t, at(i), :] = scale * r0[t, at(i), :]

    origin = block_ref[0] * LANES - HALO

    @pl.loop(0, TILES)
    def _(i):
        _, north, west = halves(i)
        scale = s[at(i), :]
        column = origin + 8 * i + sub
        inside = (column > 0) & (column < BLOCKS * LANES)
        gn[at(i), :] = jnp.where(lane == 0, 0.0, north * scale * pltpu.roll(scale, 1, 1))
        gw[at(i), :] = jnp.where(inside, west * scale * s[at(i, -1), :], 0.0)

    def sweep(src, low, high, emit, count):
        def one(i, sums):
            north, west, east = gn[at(i), :], gw[at(i), :], gw[at(i, 1), :]
            xs, gs = [], []
            for t in range(STEPS):
                x = src[t, at(i), :]
                left, right = src[t, at(i, -1), :], src[t, at(i, 1), :]
                total = north * pltpu.roll(x, 1, 1) + pltpu.roll(north * x, LANES - 1, 1)
                xs.append(x)
                gs.append(total + (west * left + east * right))
            terms = emit(i, xs, gs)
            own = (i >= HALO // 8) & (i < (HALO + LANES) // 8)
            return tuple(c + jnp.where(own, v, 0.0) for c, v in zip(sums, terms))

        zero = jnp.zeros((8, LANES), jnp.float32)
        return lax.fori_loop(low, high, one, (zero,) * count)

    def added(values):
        while len(values) > 1:
            values = [v + w for v, w in zip(values[::2], values[1::2])]
        return values[0]

    def product(left, right):
        return added([v * w for v, w in zip(left, right)])

    def every(ref, i):
        return [ref[t, at(i), :] for t in range(STEPS)]

    def put(ref, i, values):
        for t in range(STEPS):
            ref[t, at(i), :] = values[t]

    def polynomial(src, dst, bounds, emit, count):
        def start(i, xs, gs):
            put(a, i, [0.5 * (g + x) for x, g in zip(xs, gs)])
            return ()

        def middle(i, xs, gs):
            put(b, i, [g + 0.125 * v for v, g in zip(every(src, i), gs)])
            return ()

        def end(i, xs, gs):
            given = every(src, i)
            made = [g + 0.75 * v for v, g in zip(given, gs)]
            put(dst, i, made)
            return emit(i, given, made)

        sweep(src, *bounds[0], start, 0)
        sweep(a, *bounds[1], middle, 0)
        return sweep(b, *bounds[2], end, count)

    def operate(src, dst, bounds, later, emit, count):
        def act(i, xs, gs):
            inverse = s[at(i), :] * s[at(i), :]
            made = []
            for t in range(STEPS):
                other = t + 1 if later else t - 1
                value = xs[t] - gs[t]
                made.append(value - inverse * xs[other] if 0 <= other < STEPS else value)
            put(dst, i, made)
            return emit(xs, made)

        return sweep(src, *bounds, act, count)

    full, most = (0, TILES), (1, TILES - 1)
    (m0,) = polynomial(r0, q0, (full, full, full), lambda i, v, q: (product(v, q),), 1)
    (m1,) = operate(q0, r1, full, True, lambda x, r: (product(r, x[::-1]),), 1)
    (m2,) = polynomial(r1, q1, (full, most, most), lambda i, v, q: (product(v, q),), 1)
    operate(q1, r0, most, False, lambda x, r: (), 0)
    m4, m3 = polynomial(r0, q2, (most, most, most), lambda i, v, q: (product(v, q), product(every(r1, i), q[::-1])), 2)
    (m5,) = operate(q2, a, most, True, lambda x, r: (product(r, x[::-1]),), 1)

    def square(i, xs, gs):
        put(b, i, gs)
        return (added([x * (0.75 * x + 0.125 * g) + 0.5 * (g * g) for x, g in zip(xs, gs)]),)

    (m6,) = sweep(a, *most, square, 1)
    (m7,) = sweep(b, 2, TILES - 2, lambda i, xs, gs: (0.5 * product(xs, gs),), 1)

    moments = jnp.zeros((8, LANES), jnp.float32)
    for n, value in enumerate((m0, m1, m2, m3, m4, m5, m6 + m7)):
        moments = jnp.where(sub == n, jnp.sum(value, axis=0, keepdims=True), moments)
    totals = jnp.sum(moments, axis=1, keepdims=True)
    line = jnp.sum(jnp.where(lane == sub, totals, 0.0), axis=0, keepdims=True)

    own = slice(PAD + HALO, PAD + HALO + LANES)
    for t in range(STEPS):
        for field, (ref, step) in enumerate(((q0, STEPS - 1 - t), (q1, t), (q2, STEPS - 1 - t))):
            turned = (s[own, :] * ref[step, own, :]).T
            for i in range(STRIPS):
                to = BACK * (STRIPS * t + i) + 8 * field
                out_ref[to : to + 8, :] = turned[8 * i : 8 * i + 8]
    for d in range(BLOCKS):
        out_ref[BACK * d + 24 : BACK * d + 25, :] = line


def coefficients(m):
    def combined(p, q, shift):
        total = None
        for i, x in enumerate(p):
            for j, y in enumerate(q):
                if x is not None and y is not None:
                    term = x * y * m[i + j + shift]
                    total = term if total is None else total + term
        return total

    def plus(*pairs):
        made = []
        for entries in zip(*[v for _, v in pairs]):
            total = None
            for (factor, _), e in zip(pairs, entries):
                if e is not None and factor is not None:
                    total = factor * e if total is None else total + factor * e
            made.append(total)
        return made

    one = jnp.ones_like(m[0])
    nil = jnp.zeros_like(m[0])
    none = [None] * 4
    vec, vec_old = [one, None, None, None], none
    gamma, gamma_old = jnp.sqrt(m[0]), one
    w, w_old, x = none, none, none
    c = c_old = one
    s = s_old = nil
    eta = gamma
    for _ in range(3):
        z = plus((1.0 / gamma, vec))
        image = [None] + z[:3]
        delta = combined(z, z, 1)
        new = plus((one, image), (-delta / gamma, vec), (-gamma / gamma_old, vec_old))
        gamma_new = jnp.sqrt(jnp.maximum(combined(new, new, 0), 0.0))
        a0 = c * delta - c_old * s * gamma
        a1 = jnp.sqrt(a0 * a0 + gamma_new * gamma_new)
        a2 = s * delta + c_old * c * gamma
        a3 = s_old * gamma
        c_new, s_new = a0 / a1, gamma_new / a1
        w_new = plus((1.0 / a1, z), (-a3 / a1, w_old), (-a2 / a1, w))
        x = plus((one, x), (c_new * eta, w_new))
        eta = -s_new * eta
        vec_old, vec, gamma_old, gamma = vec, new, gamma, gamma_new
        w_old, w, c_old, c, s_old, s = w, w_new, c, c_new, s, s_new
    return x[:3]


def final_kernel(in_ref, out_ref):
    total = jnp.zeros((8, LANES), jnp.float32)
    for j in range(BLOCKS // 8):
        total = total + in_ref[pl.ds(24 + 8 * BACK * j, 8, stride=BACK), :]
    lane = lane_of((8, LANES))
    line = jnp.broadcast_to(jnp.sum(total, axis=0, keepdims=True), (8, LANES))
    m = [jnp.broadcast_to(jnp.sum(jnp.where(lane == n, line, 0.0), axis=1, keepdims=True), (8, LANES)) for n in range(7)]
    x0, x1, x2 = coefficients(m)
    for d in range(BLOCKS):
        at = BACK * d
        first, second, third = in_ref[at : at + 8, :], in_ref[at + 8 : at + 16, :], in_ref[at + 16 : at + 24, :]
        out_ref[:, d * LANES : (d + 1) * LANES] = x0 * first + x1 * second + x2 * third


def exchanged(blocks, rows):
    pieces = blocks.reshape(-1).reshape(BLOCKS, rows, 1, LANES)
    moved = lax.all_to_all(pieces, ("tm", "space"), split_axis=0, concat_axis=0)
    return moved.reshape(-1).reshape(BLOCKS * rows, LANES)


def body(forcing, conductivity):
    columns = forcing.shape[2]
    step = lax.axis_index("tm").astype(jnp.int32)
    block = step * STRIPS + lax.axis_index("space").astype(jnp.int32)
    scalar, whole = pl.BlockSpec(memory_space=pltpu.SMEM), pl.BlockSpec(memory_space=pltpu.VMEM)
    params = pltpu.CompilerParams(vmem_limit_bytes=40 * 2**20)
    packed = pl.pallas_call(
        pack_kernel,
        out_shape=jax.ShapeDtypeStruct((BLOCKS * SEND, LANES), jnp.float32),
        in_specs=[scalar, whole, whole],
        out_specs=whole,
        compiler_params=params,
        name="pack",
    )(step.reshape(1), forcing.reshape(8, columns), conductivity)
    flat, field = pltpu.VMEM((TALL, LANES), jnp.float32), pltpu.VMEM((STEPS, TALL, LANES), jnp.float32)
    basis = pl.pallas_call(
        main_kernel,
        out_shape=jax.ShapeDtypeStruct((BLOCKS * BACK, LANES), jnp.float32),
        in_specs=[scalar, whole],
        out_specs=whole,
        scratch_shapes=[pltpu.VMEM((LANES, LANES), jnp.float32)] + [flat] * 4 + [field] * 7,
        compiler_params=params,
        name="basis",
    )(block.reshape(1), exchanged(packed, SEND))
    out = pl.pallas_call(
        final_kernel,
        out_shape=jax.ShapeDtypeStruct((8, columns), jnp.float32),
        in_specs=[whole],
        out_specs=whole,
        compiler_params=params,
        name="combine",
    )(exchanged(basis, BACK))
    return out.reshape(1, 8, columns)


def solution(mesh):
    return jax.shard_map(
        body,
        mesh=mesh,
        in_specs=(P("tm", "space", None), P("space", None)),
        out_specs=P("tm", "space", None),
        check_vma=False,
    )
```

```python
import jax
import jax.numpy as jnp
from jax import lax
from jax.experimental import pallas as pl
from jax.experimental.pallas import tpu as pltpu
from jax.sharding import PartitionSpec as P

STEPS = 8
STRIPS = 16
BLOCKS = STEPS * STRIPS
LANES = 128
HALO = 16
WIDE = LANES + 2 * HALO
PAD = 8
TALL = WIDE + 2 * PAD
TILES = WIDE // 8
SEND = 12
BACK = 25


def lane_of(shape):
    return lax.broadcasted_iota(jnp.int32, shape, 1)


def row_of(shape):
    return lax.broadcasted_iota(jnp.int32, shape, 0)


def pack_kernel(step_ref, f_ref, k_ref, out_ref, side_ref):
    step = step_ref[0]
    shift = lax.rem(jnp.int32(48) - 32 * step + 256, jnp.int32(128))
    first, last = step == 0, step == 4
    lane = lane_of((8, LANES))
    zero = jnp.zeros((8, LANES), jnp.float32)

    def tile(ref, d):
        return ref[:, d * LANES : (d + 1) * LANES]

    def rolled(d):
        if d < 0 or d >= BLOCKS:
            return zero, zero
        return pltpu.roll(tile(f_ref, d), 16, 1), pltpu.roll(tile(k_ref, d), shift, 1)

    before, here = rolled(-1), rolled(0)
    for d in range(BLOCKS):
        after = rolled(d + 1)
        lower = jnp.where(first, before[1], here[1])
        upper = jnp.where(last, after[1], here[1])
        side_ref[8 * d : 8 * d + 8, :] = jnp.where(
            lane < 16, before[0], jnp.where(lane < 32, after[0], jnp.where(lane < 48, lower, upper))
        )
        out_ref[d * SEND : d * SEND + 8, :] = tile(f_ref, d)
        before, here = here, after
    for d in range(BLOCKS):
        upper, lower = side_ref[8 * d : 8 * d + 4, :], side_ref[8 * d + 4 : 8 * d + 8, :]
        folded = jnp.where(lane[:4] < 64, upper, pltpu.roll(lower, 64, 1))
        out_ref[d * SEND + 8 : d * SEND + 12, :] = folded


def main_kernel(block_ref, in_ref, out_ref, sides, k, s, gn, gw, r0, r1, a, b, q0, q1, q2):
    lane = lane_of((8, LANES))
    sub = row_of((8, LANES))
    edge = jnp.zeros((PAD, LANES), jnp.float32)
    edges = jnp.zeros((STEPS, PAD, LANES), jnp.float32)
    for ref in (k, s, gn, gw):
        ref[0:PAD, :] = edge
        ref[PAD + WIDE : TALL, :] = edge
    for ref in (r0, r1, a, b, q0, q1, q2):
        ref[:, 0:PAD, :] = edges
        ref[:, PAD + WIDE : TALL, :] = edges

    for t in range(STEPS):
        rows = []
        for i in range(STRIPS):
            at = SEND * (STRIPS * t + i)
            rows.append(in_ref[at : at + 8, :])
            piece = in_ref[at + 8 : at + 12, :]
            sides[8 * i : 8 * i + 4, :] = piece
            sides[8 * i + 4 : 8 * i + 8, :] = pltpu.roll(piece, 64, 1)
        r0[t, PAD + HALO : PAD + HALO + LANES, :] = jnp.concatenate(rows, 0).T
        turned = sides[...].T
        r0[t, PAD : PAD + HALO, :] = turned[0:16]
        r0[t, PAD + HALO + LANES : PAD + WIDE, :] = turned[16:32]
        if t < 5:
            k[PAD + 32 * t : PAD + 32 * t + 32, :] = turned[32:64]

    def at(i, offset=0):
        return pl.ds(pl.multiple_of(8 * i + PAD, 8) + offset, 8)

    def halves(i):
        mid = k[at(i), :]
        up = jnp.where(lane == 0, 0.0, pltpu.roll(mid, 1, 1))
        return mid, 0.5 * (mid + up), 0.5 * (mid + k[at(i, -1), :])

    @pl.loop(0, TILES, unroll=True)
    def _(i):
        mid, north, west = halves(i)
        down = jnp.where(lane == LANES - 1, 0.0, pltpu.roll(mid, LANES - 1, 1))
        south = 0.5 * (mid + down)
        east = 0.5 * (mid + k[at(i, 1), :])
        scale = 1.0 / jnp.sqrt(1.0 + north + south + west + east)
        s[at(i), :] = scale
        r0[:, at(i), :] = scale * r0[:, at(i), :]

    origin = block_ref[0] * LANES - HALO

    @pl.loop(0, TILES, unroll=True)
    def _(i):
        _, north, west = halves(i)
        scale = s[at(i), :]
        column = origin + 8 * i + sub
        inside = (column > 0) & (column < BLOCKS * LANES)
        gn[at(i), :] = jnp.where(lane == 0, 0.0, north * scale * pltpu.roll(scale, 1, 1))
        gw[at(i), :] = jnp.where(inside, west * scale * s[at(i, -1), :], 0.0)

    def sweep(src, low, high, emit, count):
        def one(i, sums):
            north, west, east = gn[at(i), :], gw[at(i), :], gw[at(i, 1), :]
            x, left, right = src[:, at(i), :], src[:, at(i, -1), :], src[:, at(i, 1), :]
            g = north * pltpu.roll(x, 1, 2) + pltpu.roll(north * x, LANES - 1, 2)
            terms = emit(i, x, g + (west * left + east * right))
            own = (i >= HALO // 8) & (i < (HALO + LANES) // 8)
            return tuple(c + jnp.where(own, jnp.sum(v, axis=0), 0.0) for c, v in zip(sums, terms))

        zero = jnp.zeros((8, LANES), jnp.float32)
        return lax.fori_loop(low, high, one, (zero,) * count, unroll=True)

    def turned_in_time(x):
        return jnp.concatenate([x[t : t + 1] for t in reversed(range(STEPS))], 0)

    def polynomial(src, dst, bounds, emit, count):
        def start(i, x, g):
            a[:, at(i), :] = 0.5 * (g + x)
            return ()

        def middle(i, x, g):
            b[:, at(i), :] = g + 0.125 * src[:, at(i), :]
            return ()

        def end(i, x, g):
            given = src[:, at(i), :]
            made = g + 0.75 * given
            dst[:, at(i), :] = made
            return emit(i, given, made)

        sweep(src, *bounds[0], start, 0)
        sweep(a, *bounds[1], middle, 0)
        return sweep(b, *bounds[2], end, count)

    def operate(src, dst, bounds, later, emit, count):
        nothing = jnp.zeros((1, 8, LANES), jnp.float32)

        def act(i, x, g):
            inverse = s[at(i), :] * s[at(i), :]
            other = jnp.concatenate([x[1:], nothing] if later else [nothing, x[:-1]], 0)
            made = x - g - inverse * other
            dst[:, at(i), :] = made
            return emit(x, made)

        return sweep(src, *bounds, act, count)

    def same(i, v, q):
        return (v * q,)

    def mirrored(x, r):
        return (r * turned_in_time(x),)

    full, most = (0, TILES), (1, TILES - 1)
    (m0,) = polynomial(r0, q0, (full, full, full), same, 1)
    (m1,) = operate(q0, r1, full, True, mirrored, 1)
    (m2,) = polynomial(r1, q1, (full, most, most), same, 1)
    operate(q1, r0, most, False, lambda x, r: (), 0)
    m4, m3 = polynomial(
        r0, q2, (most, most, most), lambda i, v, q: (v * q, r1[:, at(i), :] * turned_in_time(q)), 2
    )
    (m5,) = operate(q2, a, most, True, mirrored, 1)

    def square(i, x, g):
        b[:, at(i), :] = g
        return (x * (0.75 * x + 0.125 * g) + 0.5 * (g * g),)

    (m6,) = sweep(a, *most, square, 1)
    (m7,) = sweep(b, 2, TILES - 2, lambda i, x, g: (0.5 * (x * g),), 1)

    moments = jnp.zeros((8, LANES), jnp.float32)
    for n, value in enumerate((m0, m1, m2, m3, m4, m5, m6 + m7)):
        moments = jnp.where(sub == n, jnp.sum(value, axis=0, keepdims=True), moments)
    totals = jnp.sum(moments, axis=1, keepdims=True)
    line = jnp.sum(jnp.where(lane == sub, totals, 0.0), axis=0, keepdims=True)

    own = slice(PAD + HALO, PAD + HALO + LANES)
    for t in range(STEPS):
        for field, (ref, step) in enumerate(((q0, STEPS - 1 - t), (q1, t), (q2, STEPS - 1 - t))):
            turned = (s[own, :] * ref[step, own, :]).T
            for i in range(STRIPS):
                to = BACK * (STRIPS * t + i) + 8 * field
                out_ref[to : to + 8, :] = turned[8 * i : 8 * i + 8]
    for d in range(BLOCKS):
        out_ref[BACK * d + 24 : BACK * d + 25, :] = line


def coefficients(m):
    def combined(p, q, shift):
        total = None
        for i, x in enumerate(p):
            for j, y in enumerate(q):
                if x is not None and y is not None:
                    term = x * y * m[i + j + shift]
                    total = term if total is None else total + term
        return total

    def plus(*pairs):
        made = []
        for entries in zip(*[v for _, v in pairs]):
            total = None
            for (factor, _), e in zip(pairs, entries):
                if e is not None and factor is not None:
                    total = factor * e if total is None else total + factor * e
            made.append(total)
        return made

    one = jnp.ones_like(m[0])
    nil = jnp.zeros_like(m[0])
    none = [None] * 4
    vec, vec_old = [one, None, None, None], none
    gamma, gamma_old = jnp.sqrt(m[0]), one
    w, w_old, x = none, none, none
    c = c_old = one
    s = s_old = nil
    eta = gamma
    for _ in range(3):
        z = plus((1.0 / gamma, vec))
        image = [None] + z[:3]
        delta = combined(z, z, 1)
        new = plus((one, image), (-delta / gamma, vec), (-gamma / gamma_old, vec_old))
        gamma_new = jnp.sqrt(jnp.maximum(combined(new, new, 0), 0.0))
        a0 = c * delta - c_old * s * gamma
        a1 = jnp.sqrt(a0 * a0 + gamma_new * gamma_new)
        a2 = s * delta + c_old * c * gamma
        a3 = s_old * gamma
        c_new, s_new = a0 / a1, gamma_new / a1
        w_new = plus((1.0 / a1, z), (-a3 / a1, w_old), (-a2 / a1, w))
        x = plus((one, x), (c_new * eta, w_new))
        eta = -s_new * eta
        vec_old, vec, gamma_old, gamma = vec, new, gamma, gamma_new
        w_old, w, c_old, c, s_old, s = w, w_new, c, c_new, s, s_new
    return x[:3]


def final_kernel(in_ref, out_ref):
    total = jnp.zeros((8, LANES), jnp.float32)
    for j in range(BLOCKS // 8):
        total = total + in_ref[pl.ds(24 + 8 * BACK * j, 8, stride=BACK), :]
    lane = lane_of((8, LANES))
    line = jnp.broadcast_to(jnp.sum(total, axis=0, keepdims=True), (8, LANES))
    m = [jnp.broadcast_to(jnp.sum(jnp.where(lane == n, line, 0.0), axis=1, keepdims=True), (8, LANES)) for n in range(7)]
    x0, x1, x2 = coefficients(m)
    for d in range(BLOCKS):
        at = BACK * d
        first, second, third = in_ref[at : at + 8, :], in_ref[at + 8 : at + 16, :], in_ref[at + 16 : at + 24, :]
        out_ref[:, d * LANES : (d + 1) * LANES] = x0 * first + x1 * second + x2 * third


def exchanged(blocks, rows):
    pieces = blocks.reshape(-1).reshape(BLOCKS, rows, 1, LANES)
    moved = lax.all_to_all(pieces, ("tm", "space"), split_axis=0, concat_axis=0)
    return moved.reshape(-1).reshape(BLOCKS * rows, LANES)


def body(forcing, conductivity):
    columns = forcing.shape[2]
    step = lax.axis_index("tm").astype(jnp.int32)
    block = step * STRIPS + lax.axis_index("space").astype(jnp.int32)
    scalar, whole = pl.BlockSpec(memory_space=pltpu.SMEM), pl.BlockSpec(memory_space=pltpu.VMEM)
    params = pltpu.CompilerParams(vmem_limit_bytes=40 * 2**20)
    packed = pl.pallas_call(
        pack_kernel,
        out_shape=jax.ShapeDtypeStruct((BLOCKS * SEND, LANES), jnp.float32),
        in_specs=[scalar, whole, whole],
        out_specs=whole,
        scratch_shapes=[pltpu.VMEM((BLOCKS * 8, LANES), jnp.float32)],
        compiler_params=params,
        name="pack",
    )(step.reshape(1), forcing.reshape(8, columns), conductivity)
    flat, field = pltpu.VMEM((TALL, LANES), jnp.float32), pltpu.VMEM((STEPS, TALL, LANES), jnp.float32)
    basis = pl.pallas_call(
        main_kernel,
        out_shape=jax.ShapeDtypeStruct((BLOCKS * BACK, LANES), jnp.float32),
        in_specs=[scalar, whole],
        out_specs=whole,
        scratch_shapes=[pltpu.VMEM((LANES, LANES), jnp.float32)] + [flat] * 4 + [field] * 7,
        compiler_params=params,
        name="basis",
    )(block.reshape(1), exchanged(packed, SEND))
    out = pl.pallas_call(
        final_kernel,
        out_shape=jax.ShapeDtypeStruct((8, columns), jnp.float32),
        in_specs=[whole],
        out_specs=whole,
        compiler_params=params,
        name="combine",
    )(exchanged(basis, BACK))
    return out.reshape(1, 8, columns)


def solution(mesh):
    return jax.shard_map(
        body,
        mesh=mesh,
        in_specs=(P("tm", "space", None), P("space", None)),
        out_specs=P("tm", "space", None),
        check_vma=False,
    )
```

```python
import jax
import jax.numpy as jnp
from jax import lax
from jax.experimental import pallas as pl
from jax.experimental.pallas import tpu as pltpu
from jax.sharding import PartitionSpec as P

STEPS = 8
STRIPS = 16
BLOCKS = STEPS * STRIPS
LANES = 128
HALO = 16
WIDE = LANES + 2 * HALO
PAD = 8
TALL = WIDE + 2 * PAD
TILES = WIDE // 8
SEND = 12
BACK = 25
CHUNKS = 2
LIMIT = 60


def lane_of(shape):
    return lax.broadcasted_iota(jnp.int32, shape, 1)


def row_of(shape):
    return lax.broadcasted_iota(jnp.int32, shape, 0)


def pack_kernel(place_ref, f_hbm, k_hbm, out_ref, f_ref, k_ref, side_ref, sems):
    width = BLOCKS * LANES // CHUNKS
    copies = []
    for n in range(CHUNKS):
        part = pl.ds(n * width, width)
        copies.append(
            [
                pltpu.make_async_copy(source.at[:, part], target.at[:, part], sems.at[j, n])
                for j, (source, target) in enumerate(((f_hbm, f_ref), (k_hbm, k_ref)))
            ]
        )
    for pair in copies:
        for copy in pair:
            copy.start()

    step = place_ref[0]
    shift = lax.rem(jnp.int32(48) - 32 * step + 256, jnp.int32(128))
    first, last = step == 0, step == 4
    lane = lane_of((8, LANES))
    zero = jnp.zeros((8, LANES), jnp.float32)

    def tile(ref, d):
        return ref[:, d * LANES : (d + 1) * LANES]

    def rolled(d):
        if d < 0 or d >= BLOCKS:
            return zero, zero
        return pltpu.roll(tile(f_ref, d), 16, 1), pltpu.roll(tile(k_ref, d), shift, 1)

    before, here, done = rolled(-1), None, 0
    for n in range(CHUNKS):
        for copy in copies[n]:
            copy.wait()
        ready = BLOCKS if n == CHUNKS - 1 else (n + 1) * BLOCKS // CHUNKS - 1
        here = rolled(0) if n == 0 else here
        for d in range(done, ready):
            after = rolled(d + 1)
            lower = jnp.where(first, before[1], here[1])
            upper = jnp.where(last, after[1], here[1])
            side_ref[8 * d : 8 * d + 8, :] = jnp.where(
                lane < 16, before[0], jnp.where(lane < 32, after[0], jnp.where(lane < 48, lower, upper))
            )
            out_ref[d * SEND : d * SEND + 8, :] = tile(f_ref, d)
            before, here = here, after
        done = ready
    for d in range(BLOCKS):
        upper, lower = side_ref[8 * d : 8 * d + 4, :], side_ref[8 * d + 4 : 8 * d + 8, :]
        folded = jnp.where(lane[:4] < 64, upper, pltpu.roll(lower, 64, 1))
        out_ref[d * SEND + 8 : d * SEND + 12, :] = folded


def main_kernel(place_ref, in_ref, out_ref, sides, k, s, gn, gw, r0, r1, a, b, q0, q1, q2):
    lane = lane_of((8, LANES))
    sub = row_of((8, LANES))
    edge = jnp.zeros((PAD, LANES), jnp.float32)
    edges = jnp.zeros((STEPS, PAD, LANES), jnp.float32)
    for ref in (k, s, gn, gw):
        ref[0:PAD, :] = edge
        ref[PAD + WIDE : TALL, :] = edge
    for ref in (r0, r1, a, b, q0, q1, q2):
        ref[:, 0:PAD, :] = edges
        ref[:, PAD + WIDE : TALL, :] = edges

    for t in range(STEPS):
        rows = []
        for i in range(STRIPS):
            at = SEND * (STRIPS * t + i)
            rows.append(in_ref[at : at + 8, :])
            piece = in_ref[at + 8 : at + 12, :]
            sides[8 * i : 8 * i + 4, :] = piece
            sides[8 * i + 4 : 8 * i + 8, :] = pltpu.roll(piece, 64, 1)
        r0[t, PAD + HALO : PAD + HALO + LANES, :] = jnp.concatenate(rows, 0).T
        turned = sides[...].T
        r0[t, PAD : PAD + HALO, :] = turned[0:16]
        r0[t, PAD + HALO + LANES : PAD + WIDE, :] = turned[16:32]
        if t < 5:
            k[PAD + 32 * t : PAD + 32 * t + 32, :] = turned[32:64]

    def at(i, offset=0):
        return pl.ds(pl.multiple_of(8 * i + PAD, 8) + offset, 8)

    def halves(i):
        mid = k[at(i), :]
        up = jnp.where(lane == 0, 0.0, pltpu.roll(mid, 1, 1))
        return mid, 0.5 * (mid + up), 0.5 * (mid + k[at(i, -1), :])

    @pl.loop(0, TILES, unroll=True)
    def _(i):
        mid, north, west = halves(i)
        down = jnp.where(lane == LANES - 1, 0.0, pltpu.roll(mid, LANES - 1, 1))
        south = 0.5 * (mid + down)
        east = 0.5 * (mid + k[at(i, 1), :])
        scale = 1.0 / jnp.sqrt(1.0 + north + south + west + east)
        s[at(i), :] = scale
        r0[:, at(i), :] = scale * r0[:, at(i), :]

    origin = (place_ref[0] * STRIPS + place_ref[1]) * LANES - HALO

    @pl.loop(0, TILES, unroll=True)
    def _(i):
        _, north, west = halves(i)
        scale = s[at(i), :]
        column = origin + 8 * i + sub
        inside = (column > 0) & (column < BLOCKS * LANES)
        gn[at(i), :] = jnp.where(lane == 0, 0.0, north * scale * pltpu.roll(scale, 1, 1))
        gw[at(i), :] = jnp.where(inside, west * scale * s[at(i, -1), :], 0.0)

    def sweep(src, low, high, emit, count):
        def one(i, sums):
            north, west, east = gn[at(i), :], gw[at(i), :], gw[at(i, 1), :]
            x, left, right = src[:, at(i), :], src[:, at(i, -1), :], src[:, at(i, 1), :]
            g = north * pltpu.roll(x, 1, 2) + pltpu.roll(north * x, LANES - 1, 2)
            terms = emit(i, x, g + (west * left + east * right))
            own = (i >= HALO // 8) & (i < (HALO + LANES) // 8)
            return tuple(c + jnp.where(own, jnp.sum(v, axis=0), 0.0) for c, v in zip(sums, terms))

        zero = jnp.zeros((8, LANES), jnp.float32)
        return lax.fori_loop(low, high, one, (zero,) * count, unroll=True)

    def turned_in_time(x):
        return jnp.concatenate([x[t : t + 1] for t in reversed(range(STEPS))], 0)

    def polynomial(src, dst, bounds, emit, count):
        def start(i, x, g):
            a[:, at(i), :] = 0.5 * (g + x)
            return ()

        def middle(i, x, g):
            b[:, at(i), :] = g + 0.125 * src[:, at(i), :]
            return ()

        def end(i, x, g):
            given = src[:, at(i), :]
            made = g + 0.75 * given
            dst[:, at(i), :] = made
            return emit(i, given, made)

        sweep(src, *bounds[0], start, 0)
        sweep(a, *bounds[1], middle, 0)
        return sweep(b, *bounds[2], end, count)

    def operate(src, dst, bounds, later, emit, count):
        nothing = jnp.zeros((1, 8, LANES), jnp.float32)

        def act(i, x, g):
            inverse = s[at(i), :] * s[at(i), :]
            other = jnp.concatenate([x[1:], nothing] if later else [nothing, x[:-1]], 0)
            made = x - g - inverse * other
            dst[:, at(i), :] = made
            return emit(x, made)

        return sweep(src, *bounds, act, count)

    def same(i, v, q):
        return (v * q,)

    def mirrored(x, r):
        return (r * turned_in_time(x),)

    full, most = (0, TILES), (1, TILES - 1)
    (m0,) = polynomial(r0, q0, (full, full, full), same, 1)
    (m1,) = operate(q0, r1, full, True, mirrored, 1)
    (m2,) = polynomial(r1, q1, (full, most, most), same, 1)
    operate(q1, r0, most, False, lambda x, r: (), 0)
    m4, m3 = polynomial(
        r0, q2, (most, most, most), lambda i, v, q: (v * q, r1[:, at(i), :] * turned_in_time(q)), 2
    )
    (m5,) = operate(q2, a, most, True, mirrored, 1)

    def square(i, x, g):
        b[:, at(i), :] = g
        return (x * (0.75 * x + 0.125 * g) + 0.5 * (g * g),)

    (m6,) = sweep(a, *most, square, 1)
    (m7,) = sweep(b, 2, TILES - 2, lambda i, x, g: (0.5 * (x * g),), 1)

    moments = jnp.zeros((8, LANES), jnp.float32)
    for n, value in enumerate((m0, m1, m2, m3, m4, m5, m6 + m7)):
        moments = jnp.where(sub == n, jnp.sum(value, axis=0, keepdims=True), moments)
    totals = jnp.sum(moments, axis=1, keepdims=True)
    line = jnp.sum(jnp.where(lane == sub, totals, 0.0), axis=0, keepdims=True)

    own = slice(PAD + HALO, PAD + HALO + LANES)
    for t in range(STEPS):
        for field, (ref, step) in enumerate(((q0, STEPS - 1 - t), (q1, t), (q2, STEPS - 1 - t))):
            turned = (s[own, :] * ref[step, own, :]).T
            for i in range(STRIPS):
                to = BACK * (STRIPS * t + i) + 8 * field
                out_ref[to : to + 8, :] = turned[8 * i : 8 * i + 8]
    for d in range(BLOCKS):
        out_ref[BACK * d + 24 : BACK * d + 25, :] = line


def coefficients(m):
    def combined(p, q, shift):
        total = None
        for i, x in enumerate(p):
            for j, y in enumerate(q):
                if x is not None and y is not None:
                    term = x * y * m[i + j + shift]
                    total = term if total is None else total + term
        return total

    def plus(*pairs):
        made = []
        for entries in zip(*[v for _, v in pairs]):
            total = None
            for (factor, _), e in zip(pairs, entries):
                if e is not None and factor is not None:
                    total = factor * e if total is None else total + factor * e
            made.append(total)
        return made

    one = jnp.ones_like(m[0])
    nil = jnp.zeros_like(m[0])
    none = [None] * 4
    vec, vec_old = [one, None, None, None], none
    gamma, gamma_old = jnp.sqrt(m[0]), one
    w, w_old, x = none, none, none
    c = c_old = one
    s = s_old = nil
    eta = gamma
    for _ in range(3):
        z = plus((1.0 / gamma, vec))
        image = [None] + z[:3]
        delta = combined(z, z, 1)
        new = plus((one, image), (-delta / gamma, vec), (-gamma / gamma_old, vec_old))
        gamma_new = jnp.sqrt(jnp.maximum(combined(new, new, 0), 0.0))
        a0 = c * delta - c_old * s * gamma
        a1 = jnp.sqrt(a0 * a0 + gamma_new * gamma_new)
        a2 = s * delta + c_old * c * gamma
        a3 = s_old * gamma
        c_new, s_new = a0 / a1, gamma_new / a1
        w_new = plus((1.0 / a1, z), (-a3 / a1, w_old), (-a2 / a1, w))
        x = plus((one, x), (c_new * eta, w_new))
        eta = -s_new * eta
        vec_old, vec, gamma_old, gamma = vec, new, gamma, gamma_new
        w_old, w, c_old, c, s_old, s = w, w_new, c, c_new, s, s_new
    return x[:3]


def final_kernel(in_ref, out_ref):
    total = jnp.zeros((8, LANES), jnp.float32)
    for j in range(BLOCKS // 8):
        total = total + in_ref[pl.ds(24 + 8 * BACK * j, 8, stride=BACK), :]
    lane = lane_of((8, LANES))
    line = jnp.broadcast_to(jnp.sum(total, axis=0, keepdims=True), (8, LANES))
    m = [jnp.broadcast_to(jnp.sum(jnp.where(lane == n, line, 0.0), axis=1, keepdims=True), (8, LANES)) for n in range(7)]
    x0, x1, x2 = coefficients(m)
    for d in range(BLOCKS):
        at = BACK * d
        first, second, third = in_ref[at : at + 8, :], in_ref[at + 8 : at + 16, :], in_ref[at + 16 : at + 24, :]
        out_ref[:, d * LANES : (d + 1) * LANES] = x0 * first + x1 * second + x2 * third


def exchanged(blocks, rows):
    pieces = blocks.reshape(-1).reshape(BLOCKS, rows, 1, LANES)
    moved = lax.all_to_all(pieces, ("tm", "space"), split_axis=0, concat_axis=0)
    return moved.reshape(-1).reshape(BLOCKS * rows, LANES)


def body(forcing, conductivity):
    columns = forcing.shape[2]
    place = jnp.stack([lax.axis_index("tm"), lax.axis_index("space")]).astype(jnp.int32)
    scalar, whole = pl.BlockSpec(memory_space=pltpu.SMEM), pl.BlockSpec(memory_space=pltpu.VMEM)
    held = pl.BlockSpec(memory_space=pl.ANY)
    params = pltpu.CompilerParams(vmem_limit_bytes=40 * 2**20)
    packed = pl.pallas_call(
        pack_kernel,
        out_shape=jax.ShapeDtypeStruct((BLOCKS * SEND, LANES), jnp.float32),
        in_specs=[scalar, held, held],
        out_specs=whole,
        scratch_shapes=[
            pltpu.VMEM((8, columns), jnp.float32),
            pltpu.VMEM((8, columns), jnp.float32),
            pltpu.VMEM((BLOCKS * 8, LANES), jnp.float32),
            pltpu.SemaphoreType.DMA((2, CHUNKS)),
        ],
        compiler_params=pltpu.CompilerParams(vmem_limit_bytes=LIMIT * 2**20),
        name="pack",
    )(place, forcing.reshape(8, columns), conductivity)
    flat, field = pltpu.VMEM((TALL, LANES), jnp.float32), pltpu.VMEM((STEPS, TALL, LANES), jnp.float32)
    basis = pl.pallas_call(
        main_kernel,
        out_shape=jax.ShapeDtypeStruct((BLOCKS * BACK, LANES), jnp.float32),
        in_specs=[scalar, whole],
        out_specs=whole,
        scratch_shapes=[pltpu.VMEM((LANES, LANES), jnp.float32)] + [flat] * 4 + [field] * 7,
        compiler_params=params,
        name="basis",
    )(place, exchanged(packed, SEND))
    out = pl.pallas_call(
        final_kernel,
        out_shape=jax.ShapeDtypeStruct((8, columns), jnp.float32),
        in_specs=[whole],
        out_specs=whole,
        compiler_params=params,
        name="combine",
    )(exchanged(basis, BACK))
    return out.reshape(1, 8, columns)


def solution(mesh):
    return jax.shard_map(
        body,
        mesh=mesh,
        in_specs=(P("tm", "space", None), P("space", None)),
        out_specs=P("tm", "space", None),
        check_vma=False,
    )
```

```python
import jax
import jax.numpy as jnp
from jax import lax
from jax.experimental import pallas as pl
from jax.experimental.pallas import tpu as pltpu
from jax.sharding import PartitionSpec as P

STEPS = 8
STRIPS = 16
BLOCKS = STEPS * STRIPS
LANES = 128
HALO = 16
WIDE = LANES + 2 * HALO
PAD = 8
TALL = WIDE + 2 * PAD
TILES = WIDE // 8
SEND = 12
BACK = 25
CHUNKS = 2
PARTS = 2


def lane_of(shape):
    return lax.broadcasted_iota(jnp.int32, shape, 1)


def row_of(shape):
    return lax.broadcasted_iota(jnp.int32, shape, 0)


def pack_kernel(f_hbm, k_hbm, out_hbm, f_ref, k_ref, side_ref, out_ref, sems):
    width = BLOCKS * LANES // CHUNKS

    def incoming(n):
        part = pl.ds(n * width, width)
        pairs = ((f_hbm, f_ref), (k_hbm, k_ref))
        return [pltpu.make_async_copy(s.at[:, part], t.at[:, part], sems.at[j, n]) for j, (s, t) in enumerate(pairs)]

    def ready(n):
        return BLOCKS if n == CHUNKS - 1 else (n + 1) * BLOCKS // CHUNKS - 2

    def outgoing(n):
        low = ready(n - 1) if n else 0
        part = pl.ds(low * SEND, (ready(n) - low) * SEND)
        return pltpu.make_async_copy(out_ref.at[part], out_hbm.at[part], sems.at[2, n])

    for n in range(CHUNKS):
        for copy in incoming(n):
            copy.start()

    step = lax.axis_index("tm").astype(jnp.int32)
    shift = lax.rem(jnp.int32(48) - 32 * step + 256, jnp.int32(128))
    first, last = step == 0, step == 4
    lane = lane_of((8, LANES))
    zero = jnp.zeros((8, LANES), jnp.float32)

    def tile(ref, d):
        return ref[:, d * LANES : (d + 1) * LANES]

    def rolled(d):
        if d < 0 or d >= BLOCKS:
            return zero, zero
        return pltpu.roll(tile(f_ref, d), 16, 1), pltpu.roll(tile(k_ref, d), shift, 1)

    before, here, done = rolled(-1), None, 0
    for n in range(CHUNKS):
        for copy in incoming(n):
            copy.wait()
        here = rolled(0) if n == 0 else here
        for d in range(done, ready(n)):
            after = rolled(d + 1)
            lower = jnp.where(first, before[1], here[1])
            upper = jnp.where(last, after[1], here[1])
            side_ref[8 * d : 8 * d + 8, :] = jnp.where(
                lane < 16, before[0], jnp.where(lane < 32, after[0], jnp.where(lane < 48, lower, upper))
            )
            out_ref[d * SEND : d * SEND + 8, :] = tile(f_ref, d)
            before, here = here, after
        for d in range(done, ready(n)):
            upper, lower = side_ref[8 * d : 8 * d + 4, :], side_ref[8 * d + 4 : 8 * d + 8, :]
            folded = jnp.where(lane[:4] < 64, upper, pltpu.roll(lower, 64, 1))
            out_ref[d * SEND + 8 : d * SEND + 12, :] = folded
        done = ready(n)
        outgoing(n).start()
    for n in range(CHUNKS):
        outgoing(n).wait()


def main_kernel(in_ref, out_ref, sides, k, s, gn, gw, r0, r1, a, b, q0, q1, q2):
    lane = lane_of((8, LANES))
    sub = row_of((8, LANES))
    edge = jnp.zeros((PAD, LANES), jnp.float32)
    edges = jnp.zeros((STEPS, PAD, LANES), jnp.float32)
    for ref in (k, s, gn, gw):
        ref[0:PAD, :] = edge
        ref[PAD + WIDE : TALL, :] = edge
    for ref in (r0, r1, a, b, q0, q1, q2):
        ref[:, 0:PAD, :] = edges
        ref[:, PAD + WIDE : TALL, :] = edges

    for t in range(STEPS):
        rows = []
        for i in range(STRIPS):
            at = SEND * (STRIPS * t + i)
            rows.append(in_ref[at : at + 8, :])
            piece = in_ref[at + 8 : at + 12, :]
            sides[8 * i : 8 * i + 4, :] = piece
            sides[8 * i + 4 : 8 * i + 8, :] = pltpu.roll(piece, 64, 1)
        r0[t, PAD + HALO : PAD + HALO + LANES, :] = jnp.concatenate(rows, 0).T
        turned = sides[...].T
        r0[t, PAD : PAD + HALO, :] = turned[0:16]
        r0[t, PAD + HALO + LANES : PAD + WIDE, :] = turned[16:32]
        if t < 5:
            k[PAD + 32 * t : PAD + 32 * t + 32, :] = turned[32:64]

    def at(i, offset=0):
        return pl.ds(pl.multiple_of(8 * i + PAD, 8) + offset, 8)

    def halves(i):
        mid = k[at(i), :]
        up = jnp.where(lane == 0, 0.0, pltpu.roll(mid, 1, 1))
        return mid, 0.5 * (mid + up), 0.5 * (mid + k[at(i, -1), :])

    @pl.loop(0, TILES, unroll=True)
    def _(i):
        mid, north, west = halves(i)
        down = jnp.where(lane == LANES - 1, 0.0, pltpu.roll(mid, LANES - 1, 1))
        south = 0.5 * (mid + down)
        east = 0.5 * (mid + k[at(i, 1), :])
        scale = 1.0 / jnp.sqrt(1.0 + north + south + west + east)
        s[at(i), :] = scale
        r0[:, at(i), :] = scale * r0[:, at(i), :]

    block = lax.axis_index("tm") * STRIPS + lax.axis_index("space")
    origin = block.astype(jnp.int32) * LANES - HALO

    @pl.loop(0, TILES, unroll=True)
    def _(i):
        _, north, west = halves(i)
        scale = s[at(i), :]
        column = origin + 8 * i + sub
        inside = (column > 0) & (column < BLOCKS * LANES)
        gn[at(i), :] = jnp.where(lane == 0, 0.0, north * scale * pltpu.roll(scale, 1, 1))
        gw[at(i), :] = jnp.where(inside, west * scale * s[at(i, -1), :], 0.0)

    def sweep(src, low, high, emit, count):
        def one(i, sums):
            north, west, east = gn[at(i), :], gw[at(i), :], gw[at(i, 1), :]
            x, left, right = src[:, at(i), :], src[:, at(i, -1), :], src[:, at(i, 1), :]
            g = north * pltpu.roll(x, 1, 2) + pltpu.roll(north * x, LANES - 1, 2)
            terms = emit(i, x, g + (west * left + east * right))
            own = (i >= HALO // 8) & (i < (HALO + LANES) // 8)
            return tuple(c + jnp.where(own, jnp.sum(v, axis=0), 0.0) for c, v in zip(sums, terms))

        zero = jnp.zeros((8, LANES), jnp.float32)
        return lax.fori_loop(low, high, one, (zero,) * count, unroll=True)

    def turned_in_time(x):
        return jnp.concatenate([x[t : t + 1] for t in reversed(range(STEPS))], 0)

    def polynomial(src, dst, bounds, emit, count):
        def start(i, x, g):
            a[:, at(i), :] = 0.5 * (g + x)
            return ()

        def middle(i, x, g):
            b[:, at(i), :] = g + 0.125 * src[:, at(i), :]
            return ()

        def end(i, x, g):
            given = src[:, at(i), :]
            made = g + 0.75 * given
            dst[:, at(i), :] = made
            return emit(i, given, made)

        sweep(src, *bounds[0], start, 0)
        sweep(a, *bounds[1], middle, 0)
        return sweep(b, *bounds[2], end, count)

    def operate(src, dst, bounds, later, emit, count):
        nothing = jnp.zeros((1, 8, LANES), jnp.float32)

        def act(i, x, g):
            inverse = s[at(i), :] * s[at(i), :]
            other = jnp.concatenate([x[1:], nothing] if later else [nothing, x[:-1]], 0)
            made = x - g - inverse * other
            dst[:, at(i), :] = made
            return emit(x, made)

        return sweep(src, *bounds, act, count)

    def same(i, v, q):
        return (v * q,)

    def mirrored(x, r):
        return (r * turned_in_time(x),)

    full, most = (0, TILES), (1, TILES - 1)
    (m0,) = polynomial(r0, q0, (full, full, full), same, 1)
    (m1,) = operate(q0, r1, full, True, mirrored, 1)
    (m2,) = polynomial(r1, q1, (full, most, most), same, 1)
    operate(q1, r0, most, False, lambda x, r: (), 0)
    m4, m3 = polynomial(
        r0, q2, (most, most, most), lambda i, v, q: (v * q, r1[:, at(i), :] * turned_in_time(q)), 2
    )
    (m5,) = operate(q2, a, most, True, mirrored, 1)

    def square(i, x, g):
        b[:, at(i), :] = g
        return (x * (0.75 * x + 0.125 * g) + 0.5 * (g * g),)

    (m6,) = sweep(a, *most, square, 1)

    def edges_of(i, total):
        x = b[:, at(i), :]
        g = gn[at(i), :] * pltpu.roll(x, 1, 2) + gw[at(i), :] * b[:, at(i, -1), :]
        return total + jnp.sum(x * g, axis=0)

    m7 = lax.fori_loop(HALO // 8, (HALO + LANES) // 8, edges_of, jnp.zeros((8, LANES), jnp.float32), unroll=True)

    moments = jnp.zeros((8, LANES), jnp.float32)
    for n, value in enumerate((m0, m1, m2, m3, m4, m5, m6 + m7)):
        moments = jnp.where(sub == n, jnp.sum(value, axis=0, keepdims=True), moments)
    totals = jnp.sum(moments, axis=1, keepdims=True)
    line = jnp.sum(jnp.where(lane == sub, totals, 0.0), axis=0, keepdims=True)

    own = slice(PAD + HALO, PAD + HALO + LANES)
    for t in range(STEPS):
        for field, (ref, step) in enumerate(((q0, STEPS - 1 - t), (q1, t), (q2, STEPS - 1 - t))):
            turned = (s[own, :] * ref[step, own, :]).T
            for i in range(STRIPS):
                to = BACK * (STRIPS * t + i) + 8 * field
                out_ref[to : to + 8, :] = turned[8 * i : 8 * i + 8]
    for d in range(BLOCKS):
        out_ref[BACK * d + 24 : BACK * d + 25, :] = line


def coefficients(m):
    def combined(p, q, shift):
        total = None
        for i, x in enumerate(p):
            for j, y in enumerate(q):
                if x is not None and y is not None:
                    term = x * y * m[i + j + shift]
                    total = term if total is None else total + term
        return total

    def plus(*pairs):
        made = []
        for entries in zip(*[v for _, v in pairs]):
            total = None
            for (factor, _), e in zip(pairs, entries):
                if e is not None and factor is not None:
                    total = factor * e if total is None else total + factor * e
            made.append(total)
        return made

    one = jnp.ones_like(m[0])
    nil = jnp.zeros_like(m[0])
    none = [None] * 4
    vec, vec_old = [one, None, None, None], none
    gamma, gamma_old = jnp.sqrt(m[0]), one
    w, w_old, x = none, none, none
    c = c_old = one
    s = s_old = nil
    eta = gamma
    for _ in range(3):
        z = plus((1.0 / gamma, vec))
        image = [None] + z[:3]
        delta = combined(z, z, 1)
        new = plus((one, image), (-delta / gamma, vec), (-gamma / gamma_old, vec_old))
        gamma_new = jnp.sqrt(jnp.maximum(combined(new, new, 0), 0.0))
        a0 = c * delta - c_old * s * gamma
        a1 = jnp.sqrt(a0 * a0 + gamma_new * gamma_new)
        a2 = s * delta + c_old * c * gamma
        a3 = s_old * gamma
        c_new, s_new = a0 / a1, gamma_new / a1
        w_new = plus((1.0 / a1, z), (-a3 / a1, w_old), (-a2 / a1, w))
        x = plus((one, x), (c_new * eta, w_new))
        eta = -s_new * eta
        vec_old, vec, gamma_old, gamma = vec, new, gamma, gamma_new
        w_old, w, c_old, c, s_old, s = w, w_new, c, c_new, s, s_new
    return x[:3]


def final_kernel(in_ref, out_hbm, out_ref, sems):
    total = jnp.zeros((8, LANES), jnp.float32)
    for j in range(BLOCKS // 8):
        total = total + in_ref[pl.ds(24 + 8 * BACK * j, 8, stride=BACK), :]
    lane = lane_of((8, LANES))
    line = jnp.broadcast_to(jnp.sum(total, axis=0, keepdims=True), (8, LANES))
    m = [jnp.broadcast_to(jnp.sum(jnp.where(lane == n, line, 0.0), axis=1, keepdims=True), (8, LANES)) for n in range(7)]
    x0, x1, x2 = coefficients(m)
    width = BLOCKS // PARTS

    def outgoing(n):
        part = pl.ds(n * width * LANES, width * LANES)
        return pltpu.make_async_copy(out_ref.at[:, part], out_hbm.at[:, part], sems.at[n])

    for n in range(PARTS):
        for d in range(n * width, (n + 1) * width):
            at = BACK * d
            first, second, third = in_ref[at : at + 8, :], in_ref[at + 8 : at + 16, :], in_ref[at + 16 : at + 24, :]
            out_ref[:, d * LANES : (d + 1) * LANES] = x0 * first + x1 * second + x2 * third
        outgoing(n).start()
    for n in range(PARTS):
        outgoing(n).wait()


def exchanged(blocks, rows):
    pieces = blocks.reshape(-1).reshape(BLOCKS, rows, 1, LANES)
    moved = lax.all_to_all(pieces, ("tm", "space"), split_axis=0, concat_axis=0)
    return moved.reshape(-1).reshape(BLOCKS * rows, LANES)


def body(forcing, conductivity):
    columns = forcing.shape[2]
    whole, held = pl.BlockSpec(memory_space=pltpu.VMEM), pl.BlockSpec(memory_space=pl.ANY)
    strip = pltpu.VMEM((8, columns), jnp.float32)
    packed = pl.pallas_call(
        pack_kernel,
        out_shape=jax.ShapeDtypeStruct((BLOCKS * SEND, LANES), jnp.float32),
        in_specs=[held, held],
        out_specs=held,
        scratch_shapes=[
            strip,
            strip,
            pltpu.VMEM((BLOCKS * 8, LANES), jnp.float32),
            pltpu.VMEM((BLOCKS * SEND, LANES), jnp.float32),
            pltpu.SemaphoreType.DMA((3, CHUNKS)),
        ],
        compiler_params=pltpu.CompilerParams(vmem_limit_bytes=60 * 2**20),
        name="pack",
    )(forcing.reshape(8, columns), conductivity)
    flat, field = pltpu.VMEM((TALL, LANES), jnp.float32), pltpu.VMEM((STEPS, TALL, LANES), jnp.float32)
    basis = pl.pallas_call(
        main_kernel,
        out_shape=jax.ShapeDtypeStruct((BLOCKS * BACK, LANES), jnp.float32),
        in_specs=[whole],
        out_specs=whole,
        scratch_shapes=[pltpu.VMEM((LANES, LANES), jnp.float32)] + [flat] * 4 + [field] * 7,
        compiler_params=pltpu.CompilerParams(vmem_limit_bytes=40 * 2**20),
        name="basis",
    )(exchanged(packed, SEND))
    out = pl.pallas_call(
        final_kernel,
        out_shape=jax.ShapeDtypeStruct((8, columns), jnp.float32),
        in_specs=[whole],
        out_specs=held,
        scratch_shapes=[strip, pltpu.SemaphoreType.DMA((PARTS,))],
        compiler_params=pltpu.CompilerParams(vmem_limit_bytes=40 * 2**20),
        name="combine",
    )(exchanged(basis, BACK))
    return out.reshape(1, 8, columns)


def solution(mesh):
    return jax.shard_map(
        body,
        mesh=mesh,
        in_specs=(P("tm", "space", None), P("space", None)),
        out_specs=P("tm", "space", None),
        check_vma=False,
    )
```

```python
import jax
import jax.numpy as jnp
from jax import lax
from jax.experimental import pallas as pl
from jax.experimental.pallas import tpu as pltpu
from jax.sharding import PartitionSpec as P

STEPS = 8
STRIPS = 16
BLOCKS = STEPS * STRIPS
LANES = 128
HALO = 16
WIDE = LANES + 2 * HALO
PAD = 8
TALL = WIDE + 2 * PAD
TILES = WIDE // 8
SEND = 11
BACK = 25
CHUNKS = 2
PARTS = 2


def lane_of(shape):
    return lax.broadcasted_iota(jnp.int32, shape, 1)


def row_of(shape):
    return lax.broadcasted_iota(jnp.int32, shape, 0)


def pack_kernel(f_hbm, k_hbm, out_hbm, f_ref, k_ref, side_ref, out_ref, sems):
    step = lax.axis_index("tm").astype(jnp.int32)
    row = pltpu.make_async_copy(k_hbm.at[pl.ds(step, 1), :], k_ref, sems.at[2, 0])
    width = BLOCKS * LANES // CHUNKS

    def incoming(n):
        part = pl.ds(n * width, width)
        return pltpu.make_async_copy(f_hbm.at[:, part], f_ref.at[:, part], sems.at[0, n])

    def ready(n):
        return BLOCKS if n == CHUNKS - 1 else (n + 1) * BLOCKS // CHUNKS - 8

    def outgoing(n):
        low = ready(n - 1) if n else 0
        part = pl.ds(low * SEND, (ready(n) - low) * SEND)
        return pltpu.make_async_copy(out_ref.at[part], out_hbm.at[part], sems.at[1, n])

    row.start()
    for n in range(CHUNKS):
        incoming(n).start()

    lane = lane_of((8, LANES))
    zero = jnp.zeros((8, LANES), jnp.float32)

    def tile(ref, d):
        return ref[:, d * LANES : (d + 1) * LANES]

    def rolled(d):
        if d < 0 or d >= BLOCKS:
            return zero
        return pltpu.roll(tile(f_ref, d), 14, 1)

    def spread(d):
        if d < 0 or d >= BLOCKS:
            return zero
        return jnp.broadcast_to(tile(k_ref, d), (8, LANES))

    row.wait()
    before, here, done = rolled(-1), None, 0
    for n in range(CHUNKS):
        incoming(n).wait()
        here = rolled(0) if n == 0 else here
        for d in range(done, ready(n)):
            after = rolled(d + 1)
            beside = jnp.where(lane >= 64, spread(d - 1), spread(d + 1))
            beside = pltpu.roll(beside, 16, 1, stride=4, stride_axis=0)
            side_ref[8 * d : 8 * d + 8, :] = jnp.where(lane < 14, before, jnp.where(lane < 28, after, beside))
            out_ref[d * SEND : d * SEND + 8, :] = tile(f_ref, d)
            out_ref[d * SEND + 10 : d * SEND + 11, :] = tile(k_ref, d)
            before, here = here, after
        for d in range(done, ready(n), 4):
            group = [side_ref[pl.ds(8 * d + q, 8, stride=4), :] for q in range(4)]
            group = [group[0]] + [pltpu.roll(group[q], 32 * q, 1) for q in range(1, 4)]
            folded = jnp.where(lane < 64, jnp.where(lane < 32, *group[:2]), jnp.where(lane < 96, *group[2:]))
            for m in range(4):
                at = (d + m) * SEND + 8
                out_ref[at : at + 2, :] = folded[2 * m : 2 * m + 2]
        done = ready(n)
        outgoing(n).start()
    for n in range(CHUNKS):
        outgoing(n).wait()


def main_kernel(in_ref, out_ref, sides, k, s, gn, gw, r0, r1, a, b, q0, q1, q2):
    lane = lane_of((8, LANES))
    sub = row_of((8, LANES))
    edge = jnp.zeros((PAD, LANES), jnp.float32)
    edges = jnp.zeros((STEPS, PAD, LANES), jnp.float32)
    for ref in (k, s, gn, gw):
        ref[0:PAD, :] = edge
        ref[PAD + WIDE : TALL, :] = edge
    for ref in (r0, r1, a, b, q0, q1, q2):
        ref[:, 0:PAD, :] = edges
        ref[:, PAD + WIDE : TALL, :] = edges

    for rows in (slice(PAD, PAD + 2), slice(PAD + WIDE - 2, PAD + WIDE)):
        r0[:, rows, :] = jnp.zeros((STEPS, 2, LANES), jnp.float32)
    own = slice(PAD + HALO, PAD + HALO + LANES)
    beside = []
    for t in range(STEPS):
        base = SEND * STRIPS * t
        rows = [in_ref[base + SEND * i : base + SEND * i + 8, :] for i in range(STRIPS)]
        r0[t, own, :] = jnp.concatenate(rows, 0).T
        for j in range(2):
            groups = in_ref[pl.ds(base + 8 + j, STRIPS, stride=SEND), :]
            for q in range(4):
                sides[pl.ds(4 * j + q, STRIPS, stride=8), :] = pltpu.roll(groups, LANES - 32 * q, 1) if q else groups
        turned = sides[...].T
        r0[t, PAD + 2 : PAD + HALO, :] = turned[0:14]
        r0[t, PAD + HALO + LANES : PAD + WIDE - 2, :] = turned[14:28]
        beside.append(turned[28:32])
    rows = [in_ref[pl.ds(SEND * i + 10, 8, stride=SEND * STRIPS), :] for i in range(STRIPS)]
    k[own, :] = jnp.concatenate(rows, 0).T
    for r in range(8):
        made = jnp.zeros((4, LANES), jnp.float32)
        for t in range(STEPS):
            moved = beside[t] if t == r else pltpu.roll(beside[t], (t - r) % LANES, 1)
            made = jnp.where(lane[:4] % 8 == t, moved, made)
        v = 4 * (7 - r)
        to = PAD + v if v < HALO else PAD + LANES + v
        k[to : to + 4, :] = made

    def at(i, offset=0):
        return pl.ds(pl.multiple_of(8 * i + PAD, 8) + offset, 8)

    def halves(i):
        mid = k[at(i), :]
        up = jnp.where(lane == 0, 0.0, pltpu.roll(mid, 1, 1))
        return mid, 0.5 * (mid + up), 0.5 * (mid + k[at(i, -1), :])

    @pl.loop(0, TILES, unroll=True)
    def _(i):
        mid, north, west = halves(i)
        down = jnp.where(lane == LANES - 1, 0.0, pltpu.roll(mid, LANES - 1, 1))
        south = 0.5 * (mid + down)
        east = 0.5 * (mid + k[at(i, 1), :])
        scale = 1.0 / jnp.sqrt(1.0 + north + south + west + east)
        s[at(i), :] = scale
        r0[:, at(i), :] = scale * r0[:, at(i), :]

    block = lax.axis_index("tm") * STRIPS + lax.axis_index("space")
    origin = block.astype(jnp.int32) * LANES - HALO

    @pl.loop(0, TILES, unroll=True)
    def _(i):
        _, north, west = halves(i)
        scale = s[at(i), :]
        column = origin + 8 * i + sub
        inside = (column > 0) & (column < BLOCKS * LANES)
        gn[at(i), :] = jnp.where(lane == 0, 0.0, north * scale * pltpu.roll(scale, 1, 1))
        gw[at(i), :] = jnp.where(inside, west * scale * s[at(i, -1), :], 0.0)

    def sweep(src, low, high, emit, count):
        def one(i, sums):
            north, west, east = gn[at(i), :], gw[at(i), :], gw[at(i, 1), :]
            x, left, right = src[:, at(i), :], src[:, at(i, -1), :], src[:, at(i, 1), :]
            g = north * pltpu.roll(x, 1, 2) + pltpu.roll(north * x, LANES - 1, 2)
            terms = emit(i, x, g + (west * left + east * right))
            own = (i >= HALO // 8) & (i < (HALO + LANES) // 8)
            return tuple(c + jnp.where(own, jnp.sum(v, axis=0), 0.0) for c, v in zip(sums, terms))

        zero = jnp.zeros((8, LANES), jnp.float32)
        return lax.fori_loop(low, high, one, (zero,) * count, unroll=True)

    def turned_in_time(x):
        return jnp.concatenate([x[t : t + 1] for t in reversed(range(STEPS))], 0)

    def polynomial(src, dst, bounds, emit, count):
        def start(i, x, g):
            a[:, at(i), :] = 0.5 * (g + x)
            return ()

        def middle(i, x, g):
            b[:, at(i), :] = g + 0.125 * src[:, at(i), :]
            return ()

        def end(i, x, g):
            given = src[:, at(i), :]
            made = g + 0.75 * given
            dst[:, at(i), :] = made
            return emit(i, given, made)

        sweep(src, *bounds[0], start, 0)
        sweep(a, *bounds[1], middle, 0)
        return sweep(b, *bounds[2], end, count)

    def operate(src, dst, bounds, later, emit, count):
        nothing = jnp.zeros((1, 8, LANES), jnp.float32)

        def act(i, x, g):
            inverse = s[at(i), :] * s[at(i), :]
            other = jnp.concatenate([x[1:], nothing] if later else [nothing, x[:-1]], 0)
            made = x - g - inverse * other
            dst[:, at(i), :] = made
            return emit(x, made)

        return sweep(src, *bounds, act, count)

    def same(i, v, q):
        return (v * q,)

    def mirrored(x, r):
        return (r * turned_in_time(x),)

    full, most = (0, TILES), (1, TILES - 1)
    (m0,) = polynomial(r0, q0, (full, full, full), same, 1)
    (m1,) = operate(q0, r1, full, True, mirrored, 1)
    (m2,) = polynomial(r1, q1, (full, most, most), same, 1)
    operate(q1, r0, most, False, lambda x, r: (), 0)
    m4, m3 = polynomial(
        r0, q2, (most, most, most), lambda i, v, q: (v * q, r1[:, at(i), :] * turned_in_time(q)), 2
    )
    (m5,) = operate(q2, a, most, True, mirrored, 1)

    def square(i, x, g):
        b[:, at(i), :] = g
        return (x * (0.75 * x + 0.125 * g) + 0.5 * (g * g),)

    (m6,) = sweep(a, *most, square, 1)

    def edges_of(i, total):
        x = b[:, at(i), :]
        g = gn[at(i), :] * pltpu.roll(x, 1, 2) + gw[at(i), :] * b[:, at(i, -1), :]
        return total + jnp.sum(x * g, axis=0)

    m7 = lax.fori_loop(HALO // 8, (HALO + LANES) // 8, edges_of, jnp.zeros((8, LANES), jnp.float32), unroll=True)

    moments = jnp.zeros((8, LANES), jnp.float32)
    for n, value in enumerate((m0, m1, m2, m3, m4, m5, m6 + m7)):
        moments = jnp.where(sub == n, jnp.sum(value, axis=0, keepdims=True), moments)
    totals = jnp.sum(moments, axis=1, keepdims=True)
    line = jnp.sum(jnp.where(lane == sub, totals, 0.0), axis=0, keepdims=True)

    for t in range(STEPS):
        for field, (ref, step) in enumerate(((q0, STEPS - 1 - t), (q1, t), (q2, STEPS - 1 - t))):
            turned = (s[own, :] * ref[step, own, :]).T
            for i in range(STRIPS):
                to = BACK * (STRIPS * t + i) + 8 * field
                out_ref[to : to + 8, :] = turned[8 * i : 8 * i + 8]
    for d in range(BLOCKS):
        out_ref[BACK * d + 24 : BACK * d + 25, :] = line


def coefficients(m):
    def combined(p, q, shift):
        total = None
        for i, x in enumerate(p):
            for j, y in enumerate(q):
                if x is not None and y is not None:
                    term = x * y * m[i + j + shift]
                    total = term if total is None else total + term
        return total

    def plus(*pairs):
        made = []
        for entries in zip(*[v for _, v in pairs]):
            total = None
            for (factor, _), e in zip(pairs, entries):
                if e is not None and factor is not None:
                    total = factor * e if total is None else total + factor * e
            made.append(total)
        return made

    one = jnp.ones_like(m[0])
    nil = jnp.zeros_like(m[0])
    none = [None] * 4
    vec, vec_old = [one, None, None, None], none
    gamma, gamma_old = jnp.sqrt(m[0]), one
    w, w_old, x = none, none, none
    c = c_old = one
    s = s_old = nil
    eta = gamma
    for _ in range(3):
        z = plus((1.0 / gamma, vec))
        image = [None] + z[:3]
        delta = combined(z, z, 1)
        new = plus((one, image), (-delta / gamma, vec), (-gamma / gamma_old, vec_old))
        gamma_new = jnp.sqrt(jnp.maximum(combined(new, new, 0), 0.0))
        a0 = c * delta - c_old * s * gamma
        a1 = jnp.sqrt(a0 * a0 + gamma_new * gamma_new)
        a2 = s * delta + c_old * c * gamma
        a3 = s_old * gamma
        c_new, s_new = a0 / a1, gamma_new / a1
        w_new = plus((1.0 / a1, z), (-a3 / a1, w_old), (-a2 / a1, w))
        x = plus((one, x), (c_new * eta, w_new))
        eta = -s_new * eta
        vec_old, vec, gamma_old, gamma = vec, new, gamma, gamma_new
        w_old, w, c_old, c, s_old, s = w, w_new, c, c_new, s, s_new
    return x[:3]


def final_kernel(in_ref, out_hbm, out_ref, sems):
    total = jnp.zeros((8, LANES), jnp.float32)
    for j in range(BLOCKS // 8):
        total = total + in_ref[pl.ds(24 + 8 * BACK * j, 8, stride=BACK), :]
    lane = lane_of((8, LANES))
    line = jnp.broadcast_to(jnp.sum(total, axis=0, keepdims=True), (8, LANES))
    m = [jnp.broadcast_to(jnp.sum(jnp.where(lane == n, line, 0.0), axis=1, keepdims=True), (8, LANES)) for n in range(7)]
    x0, x1, x2 = coefficients(m)
    width = BLOCKS // PARTS

    def outgoing(n):
        part = pl.ds(n * width * LANES, width * LANES)
        return pltpu.make_async_copy(out_ref.at[:, part], out_hbm.at[:, part], sems.at[n])

    for n in range(PARTS):
        for d in range(n * width, (n + 1) * width):
            at = BACK * d
            first, second, third = in_ref[at : at + 8, :], in_ref[at + 8 : at + 16, :], in_ref[at + 16 : at + 24, :]
            out_ref[:, d * LANES : (d + 1) * LANES] = x0 * first + x1 * second + x2 * third
        outgoing(n).start()
    for n in range(PARTS):
        outgoing(n).wait()


def exchanged(blocks, rows):
    pieces = blocks.reshape(-1).reshape(BLOCKS, rows, 1, LANES)
    moved = lax.all_to_all(pieces, ("tm", "space"), split_axis=0, concat_axis=0)
    return moved.reshape(-1).reshape(BLOCKS * rows, LANES)


def body(forcing, conductivity):
    columns = forcing.shape[2]
    whole, held = pl.BlockSpec(memory_space=pltpu.VMEM), pl.BlockSpec(memory_space=pl.ANY)
    strip = pltpu.VMEM((8, columns), jnp.float32)
    packed = pl.pallas_call(
        pack_kernel,
        out_shape=jax.ShapeDtypeStruct((BLOCKS * SEND, LANES), jnp.float32),
        in_specs=[held, held],
        out_specs=held,
        scratch_shapes=[
            strip,
            pltpu.VMEM((1, columns), jnp.float32),
            pltpu.VMEM((BLOCKS * 8, LANES), jnp.float32),
            pltpu.VMEM((BLOCKS * SEND, LANES), jnp.float32),
            pltpu.SemaphoreType.DMA((3, CHUNKS)),
        ],
        compiler_params=pltpu.CompilerParams(vmem_limit_bytes=60 * 2**20),
        name="pack",
    )(forcing.reshape(8, columns), conductivity)
    flat, field = pltpu.VMEM((TALL, LANES), jnp.float32), pltpu.VMEM((STEPS, TALL, LANES), jnp.float32)
    basis = pl.pallas_call(
        main_kernel,
        out_shape=jax.ShapeDtypeStruct((BLOCKS * BACK, LANES), jnp.float32),
        in_specs=[whole],
        out_specs=whole,
        scratch_shapes=[pltpu.VMEM((LANES, LANES), jnp.float32)] + [flat] * 4 + [field] * 7,
        compiler_params=pltpu.CompilerParams(vmem_limit_bytes=40 * 2**20),
        name="basis",
    )(exchanged(packed, SEND))
    out = pl.pallas_call(
        final_kernel,
        out_shape=jax.ShapeDtypeStruct((8, columns), jnp.float32),
        in_specs=[whole],
        out_specs=held,
        scratch_shapes=[strip, pltpu.SemaphoreType.DMA((PARTS,))],
        compiler_params=pltpu.CompilerParams(vmem_limit_bytes=40 * 2**20),
        name="combine",
    )(exchanged(basis, BACK))
    return out.reshape(1, 8, columns)


def solution(mesh):
    return jax.shard_map(
        body,
        mesh=mesh,
        in_specs=(P("tm", "space", None), P("space", None)),
        out_specs=P("tm", "space", None),
        check_vma=False,
    )
```

```python
import jax
import jax.numpy as jnp
from jax import lax
from jax.experimental import pallas as pl
from jax.experimental.pallas import tpu as pltpu
from jax.sharding import PartitionSpec as P

STEPS = 8
STRIPS = 16
BLOCKS = STEPS * STRIPS
LANES = 128
HALO = 16
WIDE = LANES + 2 * HALO
PAD = 8
TALL = WIDE + 2 * PAD
TILES = WIDE // 8
SEND = 11
BACK = 25
CHUNKS = 2
PARTS = 2


def lane_of(shape):
    return lax.broadcasted_iota(jnp.int32, shape, 1)


def row_of(shape):
    return lax.broadcasted_iota(jnp.int32, shape, 0)


def pack_kernel(f_hbm, k_hbm, out_ref, f_ref, k_ref, side_ref, sems):
    step = lax.axis_index("tm").astype(jnp.int32)
    row = pltpu.make_async_copy(k_hbm.at[pl.ds(step, 1), :], k_ref, sems.at[CHUNKS])
    width = BLOCKS * LANES // CHUNKS

    def incoming(n):
        part = pl.ds(n * width, width)
        return pltpu.make_async_copy(f_hbm.at[:, part], f_ref.at[:, part], sems.at[n])

    def ready(n):
        return BLOCKS if n == CHUNKS - 1 else (n + 1) * BLOCKS // CHUNKS - 8

    row.start()
    for n in range(CHUNKS):
        incoming(n).start()

    lane = lane_of((8, LANES))
    zero = jnp.zeros((8, LANES), jnp.float32)

    def tile(ref, d):
        return ref[:, d * LANES : (d + 1) * LANES]

    def rolled(d):
        if d < 0 or d >= BLOCKS:
            return zero
        return pltpu.roll(tile(f_ref, d), 14, 1)

    def spread(d):
        if d < 0 or d >= BLOCKS:
            return zero
        return jnp.broadcast_to(tile(k_ref, d), (8, LANES))

    row.wait()
    before, here, done = rolled(-1), None, 0
    for n in range(CHUNKS):
        incoming(n).wait()
        here = rolled(0) if n == 0 else here
        for d in range(done, ready(n)):
            after = rolled(d + 1)
            beside = jnp.where(lane >= 64, spread(d - 1), spread(d + 1))
            beside = pltpu.roll(beside, 16, 1, stride=4, stride_axis=0)
            side_ref[8 * d : 8 * d + 8, :] = jnp.where(lane < 14, before, jnp.where(lane < 28, after, beside))
            out_ref[d * SEND : d * SEND + 8, :] = tile(f_ref, d)
            out_ref[d * SEND + 10 : d * SEND + 11, :] = tile(k_ref, d)
            before, here = here, after
        for d in range(done, ready(n), 4):
            group = [side_ref[pl.ds(8 * d + q, 8, stride=4), :] for q in range(4)]
            group = [group[0]] + [pltpu.roll(group[q], 32 * q, 1) for q in range(1, 4)]
            folded = jnp.where(lane < 64, jnp.where(lane < 32, *group[:2]), jnp.where(lane < 96, *group[2:]))
            for m in range(4):
                at = (d + m) * SEND + 8
                out_ref[at : at + 2, :] = folded[2 * m : 2 * m + 2]
        done = ready(n)


def main_kernel(in_ref, out_ref, sides, k, s, gn, gw, r0, r1, a, b, q0, q1, q2):
    lane = lane_of((8, LANES))
    sub = row_of((8, LANES))
    edge = jnp.zeros((PAD, LANES), jnp.float32)
    edges = jnp.zeros((STEPS, PAD, LANES), jnp.float32)
    for ref in (k, s, gn, gw):
        ref[0:PAD, :] = edge
        ref[PAD + WIDE : TALL, :] = edge
    for ref in (r0, r1, a, b, q0, q1, q2):
        ref[:, 0:PAD, :] = edges
        ref[:, PAD + WIDE : TALL, :] = edges

    for rows in (slice(PAD, PAD + 2), slice(PAD + WIDE - 2, PAD + WIDE)):
        r0[:, rows, :] = jnp.zeros((STEPS, 2, LANES), jnp.float32)
    own = slice(PAD + HALO, PAD + HALO + LANES)
    beside = []
    for t in range(STEPS):
        base = SEND * STRIPS * t
        rows = [in_ref[base + SEND * i : base + SEND * i + 8, :] for i in range(STRIPS)]
        r0[t, own, :] = jnp.concatenate(rows, 0).T
        for j in range(2):
            groups = in_ref[pl.ds(base + 8 + j, STRIPS, stride=SEND), :]
            for q in range(4):
                sides[pl.ds(4 * j + q, STRIPS, stride=8), :] = pltpu.roll(groups, LANES - 32 * q, 1) if q else groups
        turned = sides[...].T
        r0[t, PAD + 2 : PAD + HALO, :] = turned[0:14]
        r0[t, PAD + HALO + LANES : PAD + WIDE - 2, :] = turned[14:28]
        beside.append(turned[28:32])
    rows = [in_ref[pl.ds(SEND * i + 10, 8, stride=SEND * STRIPS), :] for i in range(STRIPS)]
    k[own, :] = jnp.concatenate(rows, 0).T
    for r in range(8):
        made = jnp.zeros((4, LANES), jnp.float32)
        for t in range(STEPS):
            moved = beside[t] if t == r else pltpu.roll(beside[t], (t - r) % LANES, 1)
            made = jnp.where(lane[:4] % 8 == t, moved, made)
        v = 4 * (7 - r)
        to = PAD + v if v < HALO else PAD + LANES + v
        k[to : to + 4, :] = made

    def at(i, offset=0):
        return pl.ds(pl.multiple_of(8 * i + PAD, 8) + offset, 8)

    def halves(i):
        mid = k[at(i), :]
        up = jnp.where(lane == 0, 0.0, pltpu.roll(mid, 1, 1))
        return mid, 0.5 * (mid + up), 0.5 * (mid + k[at(i, -1), :])

    @pl.loop(0, TILES, unroll=True)
    def _(i):
        mid, north, west = halves(i)
        down = jnp.where(lane == LANES - 1, 0.0, pltpu.roll(mid, LANES - 1, 1))
        south = 0.5 * (mid + down)
        east = 0.5 * (mid + k[at(i, 1), :])
        scale = 1.0 / jnp.sqrt(1.0 + north + south + west + east)
        s[at(i), :] = scale
        r0[:, at(i), :] = scale * r0[:, at(i), :]

    block = lax.axis_index("tm") * STRIPS + lax.axis_index("space")
    origin = block.astype(jnp.int32) * LANES - HALO

    @pl.loop(0, TILES, unroll=True)
    def _(i):
        _, north, west = halves(i)
        scale = s[at(i), :]
        column = origin + 8 * i + sub
        inside = (column > 0) & (column < BLOCKS * LANES)
        gn[at(i), :] = jnp.where(lane == 0, 0.0, north * scale * pltpu.roll(scale, 1, 1))
        gw[at(i), :] = jnp.where(inside, west * scale * s[at(i, -1), :], 0.0)

    def sweep(src, low, high, emit, count):
        def one(i, sums):
            north, west, east = gn[at(i), :], gw[at(i), :], gw[at(i, 1), :]
            x, left, right = src[:, at(i), :], src[:, at(i, -1), :], src[:, at(i, 1), :]
            g = north * pltpu.roll(x, 1, 2) + pltpu.roll(north * x, LANES - 1, 2)
            terms = emit(i, x, g + (west * left + east * right))
            own = (i >= HALO // 8) & (i < (HALO + LANES) // 8)
            return tuple(c + jnp.where(own, jnp.sum(v, axis=0), 0.0) for c, v in zip(sums, terms))

        zero = jnp.zeros((8, LANES), jnp.float32)
        return lax.fori_loop(low, high, one, (zero,) * count, unroll=True)

    def turned_in_time(x):
        return jnp.concatenate([x[t : t + 1] for t in reversed(range(STEPS))], 0)

    def polynomial(src, dst, bounds, emit, count):
        def start(i, x, g):
            a[:, at(i), :] = 0.5 * (g + x)
            return ()

        def middle(i, x, g):
            b[:, at(i), :] = g + 0.125 * src[:, at(i), :]
            return ()

        def end(i, x, g):
            given = src[:, at(i), :]
            made = g + 0.75 * given
            dst[:, at(i), :] = made
            return emit(i, given, made)

        sweep(src, *bounds[0], start, 0)
        sweep(a, *bounds[1], middle, 0)
        return sweep(b, *bounds[2], end, count)

    def operate(src, dst, bounds, later, emit, count):
        nothing = jnp.zeros((1, 8, LANES), jnp.float32)

        def act(i, x, g):
            inverse = s[at(i), :] * s[at(i), :]
            other = jnp.concatenate([x[1:], nothing] if later else [nothing, x[:-1]], 0)
            made = x - g - inverse * other
            dst[:, at(i), :] = made
            return emit(x, made)

        return sweep(src, *bounds, act, count)

    def same(i, v, q):
        return (v * q,)

    def mirrored(x, r):
        return (r * turned_in_time(x),)

    full, most = (0, TILES), (1, TILES - 1)
    (m0,) = polynomial(r0, q0, (full, full, full), same, 1)
    (m1,) = operate(q0, r1, full, True, mirrored, 1)
    (m2,) = polynomial(r1, q1, (full, most, most), same, 1)
    operate(q1, r0, most, False, lambda x, r: (), 0)
    m4, m3 = polynomial(
        r0, q2, (most, most, most), lambda i, v, q: (v * q, r1[:, at(i), :] * turned_in_time(q)), 2
    )
    (m5,) = operate(q2, a, most, True, mirrored, 1)

    def square(i, x, g):
        b[:, at(i), :] = g
        return (x * (0.75 * x + 0.125 * g) + 0.5 * (g * g),)

    (m6,) = sweep(a, *most, square, 1)

    def edges_of(i, total):
        x = b[:, at(i), :]
        g = gn[at(i), :] * pltpu.roll(x, 1, 2) + gw[at(i), :] * b[:, at(i, -1), :]
        return total + jnp.sum(x * g, axis=0)

    m7 = lax.fori_loop(HALO // 8, (HALO + LANES) // 8, edges_of, jnp.zeros((8, LANES), jnp.float32), unroll=True)

    moments = jnp.zeros((8, LANES), jnp.float32)
    for n, value in enumerate((m0, m1, m2, m3, m4, m5, m6 + m7)):
        moments = jnp.where(sub == n, jnp.sum(value, axis=0, keepdims=True), moments)
    totals = jnp.sum(moments, axis=1, keepdims=True)
    line = jnp.sum(jnp.where(lane == sub, totals, 0.0), axis=0, keepdims=True)

    for t in range(STEPS):
        for field, (ref, step) in enumerate(((q0, STEPS - 1 - t), (q1, t), (q2, STEPS - 1 - t))):
            turned = (s[own, :] * ref[step, own, :]).T
            for i in range(STRIPS):
                to = BACK * (STRIPS * t + i) + 8 * field
                out_ref[to : to + 8, :] = turned[8 * i : 8 * i + 8]
    for d in range(BLOCKS):
        out_ref[BACK * d + 24 : BACK * d + 25, :] = line


def coefficients(m):
    def combined(p, q, shift):
        total = None
        for i, x in enumerate(p):
            for j, y in enumerate(q):
                if x is not None and y is not None:
                    term = x * y * m[i + j + shift]
                    total = term if total is None else total + term
        return total

    def plus(*pairs):
        made = []
        for entries in zip(*[v for _, v in pairs]):
            total = None
            for (factor, _), e in zip(pairs, entries):
                if e is not None and factor is not None:
                    total = factor * e if total is None else total + factor * e
            made.append(total)
        return made

    one = jnp.ones_like(m[0])
    nil = jnp.zeros_like(m[0])
    none = [None] * 4
    vec, vec_old = [one, None, None, None], none
    gamma, gamma_old = jnp.sqrt(m[0]), one
    w, w_old, x = none, none, none
    c = c_old = one
    s = s_old = nil
    eta = gamma
    for _ in range(3):
        z = plus((1.0 / gamma, vec))
        image = [None] + z[:3]
        delta = combined(z, z, 1)
        new = plus((one, image), (-delta / gamma, vec), (-gamma / gamma_old, vec_old))
        gamma_new = jnp.sqrt(jnp.maximum(combined(new, new, 0), 0.0))
        a0 = c * delta - c_old * s * gamma
        a1 = jnp.sqrt(a0 * a0 + gamma_new * gamma_new)
        a2 = s * delta + c_old * c * gamma
        a3 = s_old * gamma
        c_new, s_new = a0 / a1, gamma_new / a1
        w_new = plus((1.0 / a1, z), (-a3 / a1, w_old), (-a2 / a1, w))
        x = plus((one, x), (c_new * eta, w_new))
        eta = -s_new * eta
        vec_old, vec, gamma_old, gamma = vec, new, gamma, gamma_new
        w_old, w, c_old, c, s_old, s = w, w_new, c, c_new, s, s_new
    return x[:3]


def final_kernel(in_ref, out_hbm, out_ref, sems):
    total = jnp.zeros((8, LANES), jnp.float32)
    for j in range(BLOCKS // 8):
        total = total + in_ref[pl.ds(24 + 8 * BACK * j, 8, stride=BACK), :]
    lane = lane_of((8, LANES))
    line = jnp.broadcast_to(jnp.sum(total, axis=0, keepdims=True), (8, LANES))
    m = [jnp.broadcast_to(jnp.sum(jnp.where(lane == n, line, 0.0), axis=1, keepdims=True), (8, LANES)) for n in range(7)]
    x0, x1, x2 = coefficients(m)
    width = BLOCKS // PARTS

    def outgoing(n):
        part = pl.ds(n * width * LANES, width * LANES)
        return pltpu.make_async_copy(out_ref.at[:, part], out_hbm.at[:, part], sems.at[n])

    for n in range(PARTS):
        for d in range(n * width, (n + 1) * width):
            at = BACK * d
            first, second, third = in_ref[at : at + 8, :], in_ref[at + 8 : at + 16, :], in_ref[at + 16 : at + 24, :]
            out_ref[:, d * LANES : (d + 1) * LANES] = x0 * first + x1 * second + x2 * third
        outgoing(n).start()
    for n in range(PARTS):
        outgoing(n).wait()


def exchanged(blocks, rows):
    pieces = blocks.reshape(-1).reshape(BLOCKS, rows, 1, LANES)
    moved = lax.all_to_all(pieces, ("tm", "space"), split_axis=0, concat_axis=0)
    return moved.reshape(-1).reshape(BLOCKS * rows, LANES)


def in_hbm(array):
    return pltpu.with_memory_space_constraint(array, pltpu.HBM)


def body(forcing, conductivity):
    columns = forcing.shape[2]
    whole, held = pl.BlockSpec(memory_space=pltpu.VMEM), pl.BlockSpec(memory_space=pl.ANY)
    strip = pltpu.VMEM((8, columns), jnp.float32)
    packed = pl.pallas_call(
        pack_kernel,
        out_shape=pltpu.VMEM((BLOCKS * SEND, LANES), jnp.float32),
        in_specs=[held, held],
        out_specs=whole,
        scratch_shapes=[
            strip,
            pltpu.VMEM((1, columns), jnp.float32),
            pltpu.VMEM((BLOCKS * 8, LANES), jnp.float32),
            pltpu.SemaphoreType.DMA((CHUNKS + 1,)),
        ],
        compiler_params=pltpu.CompilerParams(vmem_limit_bytes=40 * 2**20),
        name="pack",
    )(in_hbm(forcing.reshape(8, columns)), in_hbm(conductivity))
    flat, field = pltpu.VMEM((TALL, LANES), jnp.float32), pltpu.VMEM((STEPS, TALL, LANES), jnp.float32)
    basis = pl.pallas_call(
        main_kernel,
        out_shape=jax.ShapeDtypeStruct((BLOCKS * BACK, LANES), jnp.float32),
        in_specs=[whole],
        out_specs=whole,
        scratch_shapes=[pltpu.VMEM((LANES, LANES), jnp.float32)] + [flat] * 4 + [field] * 7,
        compiler_params=pltpu.CompilerParams(vmem_limit_bytes=40 * 2**20),
        name="basis",
    )(exchanged(packed, SEND))
    out = pl.pallas_call(
        final_kernel,
        out_shape=jax.ShapeDtypeStruct((8, columns), jnp.float32),
        in_specs=[whole],
        out_specs=held,
        scratch_shapes=[strip, pltpu.SemaphoreType.DMA((PARTS,))],
        compiler_params=pltpu.CompilerParams(vmem_limit_bytes=40 * 2**20),
        name="combine",
    )(exchanged(basis, BACK))
    return out.reshape(1, 8, columns)


def solution(mesh):
    return jax.shard_map(
        body,
        mesh=mesh,
        in_specs=(P("tm", "space", None), P("space", None)),
        out_specs=P("tm", "space", None),
        check_vma=False,
    )
```

```python
import jax
import jax.numpy as jnp
from jax import lax
from jax.experimental import pallas as pl
from jax.experimental.pallas import tpu as pltpu
from jax.sharding import PartitionSpec as P

STEPS = 8
STRIPS = 16
BLOCKS = STEPS * STRIPS
LANES = 128
HALO = 16
WIDE = LANES + 2 * HALO
PAD = 8
TALL = WIDE + 2 * PAD
TILES = WIDE // 8
SEND = 11
BACK = 25
CHUNKS = 1
PARTS = 2


def lane_of(shape):
    return lax.broadcasted_iota(jnp.int32, shape, 1)


def row_of(shape):
    return lax.broadcasted_iota(jnp.int32, shape, 0)


def pack_kernel(f_hbm, k_hbm, out_ref, f_ref, k_ref, side_ref, sems):
    step = lax.axis_index("tm").astype(jnp.int32)
    row = pltpu.make_async_copy(k_hbm.at[pl.ds(step, 1), :], k_ref, sems.at[CHUNKS])
    width = BLOCKS * LANES // CHUNKS

    def incoming(n):
        part = pl.ds(n * width, width)
        return pltpu.make_async_copy(f_hbm.at[:, part], f_ref.at[:, part], sems.at[n])

    def ready(n):
        return BLOCKS if n == CHUNKS - 1 else (n + 1) * BLOCKS // CHUNKS - 8

    row.start()
    for n in range(CHUNKS):
        incoming(n).start()

    lane = lane_of((8, LANES))
    zero = jnp.zeros((8, LANES), jnp.float32)

    def tile(ref, d):
        return ref[:, d * LANES : (d + 1) * LANES]

    def rolled(d):
        if d < 0 or d >= BLOCKS:
            return zero
        return pltpu.roll(tile(f_ref, d), 14, 1)

    def spread(d):
        if d < 0 or d >= BLOCKS:
            return zero
        return jnp.broadcast_to(tile(k_ref, d), (8, LANES))

    row.wait()
    before, here, done = rolled(-1), None, 0
    for n in range(CHUNKS):
        incoming(n).wait()
        here = rolled(0) if n == 0 else here
        for d in range(done, ready(n)):
            after = rolled(d + 1)
            beside = jnp.where(lane >= 64, spread(d - 1), spread(d + 1))
            beside = pltpu.roll(beside, 16, 1, stride=4, stride_axis=0)
            side_ref[8 * d : 8 * d + 8, :] = jnp.where(lane < 14, before, jnp.where(lane < 28, after, beside))
            out_ref[d * SEND : d * SEND + 8, :] = tile(f_ref, d)
            out_ref[d * SEND + 10 : d * SEND + 11, :] = tile(k_ref, d)
            before, here = here, after
        for d in range(done, ready(n), 4):
            group = [side_ref[pl.ds(8 * d + q, 8, stride=4), :] for q in range(4)]
            group = [group[0]] + [pltpu.roll(group[q], 32 * q, 1) for q in range(1, 4)]
            folded = jnp.where(lane < 64, jnp.where(lane < 32, *group[:2]), jnp.where(lane < 96, *group[2:]))
            for m in range(4):
                at = (d + m) * SEND + 8
                out_ref[at : at + 2, :] = folded[2 * m : 2 * m + 2]
        done = ready(n)


def main_kernel(in_ref, out_ref, sides, k, s, gn, gw, r0, r1, a, b, q0, q1, q2):
    lane = lane_of((8, LANES))
    sub = row_of((8, LANES))
    edge = jnp.zeros((PAD, LANES), jnp.float32)
    edges = jnp.zeros((STEPS, PAD, LANES), jnp.float32)
    for ref in (k, s, gn, gw):
        ref[0:PAD, :] = edge
        ref[PAD + WIDE : TALL, :] = edge
    for ref in (r0, r1, a, b, q0, q1, q2):
        ref[:, 0:PAD, :] = edges
        ref[:, PAD + WIDE : TALL, :] = edges

    for rows in (slice(PAD, PAD + 2), slice(PAD + WIDE - 2, PAD + WIDE)):
        r0[:, rows, :] = jnp.zeros((STEPS, 2, LANES), jnp.float32)
    own = slice(PAD + HALO, PAD + HALO + LANES)
    beside = []
    wide = lane_of((STRIPS, LANES))
    for low in range(0, STEPS, 4):
        for t in range(low, low + 4):
            base = SEND * STRIPS * t
            rows = [in_ref[base + SEND * i : base + SEND * i + 8, :] for i in range(STRIPS)]
            r0[t, own, :] = jnp.concatenate(rows, 0).T
        for j in range(2):
            packed = [in_ref[pl.ds(SEND * STRIPS * (low + m) + 8 + j, STRIPS, stride=SEND), :] for m in range(4)]
            for q in range(4):
                moved = [v if m == q else pltpu.roll(v, 32 * (m - q) % LANES, 1) for m, v in enumerate(packed)]
                joined = jnp.where(wide < 64, jnp.where(wide < 32, *moved[:2]), jnp.where(wide < 96, *moved[2:]))
                sides[pl.ds(4 * j + q, STRIPS, stride=8), :] = joined
        turned = sides[...].T
        for m in range(4):
            r0[low + m, PAD + 2 : PAD + HALO, :] = turned[32 * m : 32 * m + 14]
            r0[low + m, PAD + HALO + LANES : PAD + WIDE - 2, :] = turned[32 * m + 14 : 32 * m + 28]
            beside.append(turned[32 * m + 28 : 32 * m + 32])
    rows = [in_ref[pl.ds(SEND * i + 10, 8, stride=SEND * STRIPS), :] for i in range(STRIPS)]
    k[own, :] = jnp.concatenate(rows, 0).T
    for r in range(8):
        made = jnp.zeros((4, LANES), jnp.float32)
        for t in range(STEPS):
            moved = beside[t] if t == r else pltpu.roll(beside[t], (t - r) % LANES, 1)
            made = jnp.where(lane[:4] % 8 == t, moved, made)
        v = 4 * (7 - r)
        to = PAD + v if v < HALO else PAD + LANES + v
        k[to : to + 4, :] = made

    def at(i, offset=0):
        return pl.ds(pl.multiple_of(8 * i + PAD, 8) + offset, 8)

    def halves(i):
        mid = k[at(i), :]
        up = jnp.where(lane == 0, 0.0, pltpu.roll(mid, 1, 1))
        return mid, 0.5 * (mid + up), 0.5 * (mid + k[at(i, -1), :])

    @pl.loop(0, TILES, unroll=True)
    def _(i):
        mid, north, west = halves(i)
        down = jnp.where(lane == LANES - 1, 0.0, pltpu.roll(mid, LANES - 1, 1))
        south = 0.5 * (mid + down)
        east = 0.5 * (mid + k[at(i, 1), :])
        scale = 1.0 / jnp.sqrt(1.0 + north + south + west + east)
        s[at(i), :] = scale
        r0[:, at(i), :] = scale * r0[:, at(i), :]

    block = lax.axis_index("tm") * STRIPS + lax.axis_index("space")
    origin = block.astype(jnp.int32) * LANES - HALO

    @pl.loop(0, TILES, unroll=True)
    def _(i):
        _, north, west = halves(i)
        scale = s[at(i), :]
        column = origin + 8 * i + sub
        inside = (column > 0) & (column < BLOCKS * LANES)
        gn[at(i), :] = jnp.where(lane == 0, 0.0, north * scale * pltpu.roll(scale, 1, 1))
        gw[at(i), :] = jnp.where(inside, west * scale * s[at(i, -1), :], 0.0)

    def sweep(src, low, high, emit, count):
        def one(i, sums):
            north, west, east = gn[at(i), :], gw[at(i), :], gw[at(i, 1), :]
            x, left, right = src[:, at(i), :], src[:, at(i, -1), :], src[:, at(i, 1), :]
            g = north * pltpu.roll(x, 1, 2) + pltpu.roll(north * x, LANES - 1, 2)
            terms = emit(i, x, g + (west * left + east * right))
            own = (i >= HALO // 8) & (i < (HALO + LANES) // 8)
            return tuple(c + jnp.where(own, jnp.sum(v, axis=0), 0.0) for c, v in zip(sums, terms))

        zero = jnp.zeros((8, LANES), jnp.float32)
        return lax.fori_loop(low, high, one, (zero,) * count, unroll=True)

    def turned_in_time(x):
        return jnp.concatenate([x[t : t + 1] for t in reversed(range(STEPS))], 0)

    def polynomial(src, dst, bounds, emit, count):
        def start(i, x, g):
            a[:, at(i), :] = 0.5 * (g + x)
            return ()

        def middle(i, x, g):
            b[:, at(i), :] = g + 0.125 * src[:, at(i), :]
            return ()

        def end(i, x, g):
            given = src[:, at(i), :]
            made = g + 0.75 * given
            dst[:, at(i), :] = made
            return emit(i, given, made)

        sweep(src, *bounds[0], start, 0)
        sweep(a, *bounds[1], middle, 0)
        return sweep(b, *bounds[2], end, count)

    def operate(src, dst, bounds, later, emit, count):
        nothing = jnp.zeros((1, 8, LANES), jnp.float32)

        def act(i, x, g):
            inverse = s[at(i), :] * s[at(i), :]
            other = jnp.concatenate([x[1:], nothing] if later else [nothing, x[:-1]], 0)
            made = x - g - inverse * other
            dst[:, at(i), :] = made
            return emit(x, made)

        return sweep(src, *bounds, act, count)

    def same(i, v, q):
        return (v * q,)

    def mirrored(x, r):
        return (r * turned_in_time(x),)

    full, most = (0, TILES), (1, TILES - 1)
    (m0,) = polynomial(r0, q0, (full, full, full), same, 1)
    (m1,) = operate(q0, r1, full, True, mirrored, 1)
    (m2,) = polynomial(r1, q1, (full, most, most), same, 1)
    operate(q1, r0, most, False, lambda x, r: (), 0)
    m4, m3 = polynomial(
        r0, q2, (most, most, most), lambda i, v, q: (v * q, r1[:, at(i), :] * turned_in_time(q)), 2
    )
    (m5,) = operate(q2, a, most, True, mirrored, 1)

    def square(i, x, g):
        b[:, at(i), :] = g
        return (x * (0.75 * x + 0.125 * g) + 0.5 * (g * g),)

    (m6,) = sweep(a, *most, square, 1)

    def edges_of(i, total):
        x = b[:, at(i), :]
        g = gn[at(i), :] * pltpu.roll(x, 1, 2) + gw[at(i), :] * b[:, at(i, -1), :]
        return total + jnp.sum(x * g, axis=0)

    m7 = lax.fori_loop(HALO // 8, (HALO + LANES) // 8, edges_of, jnp.zeros((8, LANES), jnp.float32), unroll=True)

    moments = jnp.zeros((8, LANES), jnp.float32)
    for n, value in enumerate((m0, m1, m2, m3, m4, m5, m6 + m7)):
        moments = jnp.where(sub == n, jnp.sum(value, axis=0, keepdims=True), moments)
    totals = jnp.sum(moments, axis=1, keepdims=True)
    line = jnp.sum(jnp.where(lane == sub, totals, 0.0), axis=0, keepdims=True)

    for t in range(STEPS):
        for field, (ref, step) in enumerate(((q0, STEPS - 1 - t), (q1, t), (q2, STEPS - 1 - t))):
            turned = (s[own, :] * ref[step, own, :]).T
            for i in range(STRIPS):
                to = BACK * (STRIPS * t + i) + 8 * field
                out_ref[to : to + 8, :] = turned[8 * i : 8 * i + 8]
    for d in range(BLOCKS):
        out_ref[BACK * d + 24 : BACK * d + 25, :] = line


def coefficients(m):
    def combined(p, q, shift):
        total = None
        for i, x in enumerate(p):
            for j, y in enumerate(q):
                if x is not None and y is not None:
                    term = x * y * m[i + j + shift]
                    total = term if total is None else total + term
        return total

    def plus(*pairs):
        made = []
        for entries in zip(*[v for _, v in pairs]):
            total = None
            for (factor, _), e in zip(pairs, entries):
                if e is not None and factor is not None:
                    total = factor * e if total is None else total + factor * e
            made.append(total)
        return made

    one = jnp.ones_like(m[0])
    nil = jnp.zeros_like(m[0])
    none = [None] * 4
    vec, vec_old = [one, None, None, None], none
    gamma, gamma_old = jnp.sqrt(m[0]), one
    w, w_old, x = none, none, none
    c = c_old = one
    s = s_old = nil
    eta = gamma
    for _ in range(3):
        z = plus((1.0 / gamma, vec))
        image = [None] + z[:3]
        delta = combined(z, z, 1)
        new = plus((one, image), (-delta / gamma, vec), (-gamma / gamma_old, vec_old))
        gamma_new = jnp.sqrt(jnp.maximum(combined(new, new, 0), 0.0))
        a0 = c * delta - c_old * s * gamma
        a1 = jnp.sqrt(a0 * a0 + gamma_new * gamma_new)
        a2 = s * delta + c_old * c * gamma
        a3 = s_old * gamma
        c_new, s_new = a0 / a1, gamma_new / a1
        w_new = plus((1.0 / a1, z), (-a3 / a1, w_old), (-a2 / a1, w))
        x = plus((one, x), (c_new * eta, w_new))
        eta = -s_new * eta
        vec_old, vec, gamma_old, gamma = vec, new, gamma, gamma_new
        w_old, w, c_old, c, s_old, s = w, w_new, c, c_new, s, s_new
    return x[:3]


def final_kernel(in_ref, out_hbm, out_ref, sems):
    total = jnp.zeros((8, LANES), jnp.float32)
    for j in range(BLOCKS // 8):
        total = total + in_ref[pl.ds(24 + 8 * BACK * j, 8, stride=BACK), :]
    lane = lane_of((8, LANES))
    line = jnp.broadcast_to(jnp.sum(total, axis=0, keepdims=True), (8, LANES))
    m = [jnp.broadcast_to(jnp.sum(jnp.where(lane == n, line, 0.0), axis=1, keepdims=True), (8, LANES)) for n in range(7)]
    x0, x1, x2 = coefficients(m)
    width = BLOCKS // PARTS

    def outgoing(n):
        part = pl.ds(n * width * LANES, width * LANES)
        return pltpu.make_async_copy(out_ref.at[:, part], out_hbm.at[:, part], sems.at[n])

    for n in range(PARTS):
        for d in range(n * width, (n + 1) * width):
            at = BACK * d
            first, second, third = in_ref[at : at + 8, :], in_ref[at + 8 : at + 16, :], in_ref[at + 16 : at + 24, :]
            out_ref[:, d * LANES : (d + 1) * LANES] = x0 * first + x1 * second + x2 * third
        outgoing(n).start()
    for n in range(PARTS):
        outgoing(n).wait()


def exchanged(blocks, rows):
    pieces = blocks.reshape(-1).reshape(BLOCKS, rows, 1, LANES)
    moved = lax.all_to_all(pieces, ("tm", "space"), split_axis=0, concat_axis=0)
    return moved.reshape(-1).reshape(BLOCKS * rows, LANES)


def in_hbm(array):
    return pltpu.with_memory_space_constraint(array, pltpu.HBM)


def body(forcing, conductivity):
    columns = forcing.shape[2]
    whole, held = pl.BlockSpec(memory_space=pltpu.VMEM), pl.BlockSpec(memory_space=pl.ANY)
    strip = pltpu.VMEM((8, columns), jnp.float32)
    packed = pl.pallas_call(
        pack_kernel,
        out_shape=pltpu.VMEM((BLOCKS * SEND, LANES), jnp.float32),
        in_specs=[held, held],
        out_specs=whole,
        scratch_shapes=[
            strip,
            pltpu.VMEM((1, columns), jnp.float32),
            pltpu.VMEM((BLOCKS * 8, LANES), jnp.float32),
            pltpu.SemaphoreType.DMA((CHUNKS + 1,)),
        ],
        compiler_params=pltpu.CompilerParams(vmem_limit_bytes=40 * 2**20),
        name="pack",
    )(in_hbm(forcing.reshape(8, columns)), in_hbm(conductivity))
    flat, field = pltpu.VMEM((TALL, LANES), jnp.float32), pltpu.VMEM((STEPS, TALL, LANES), jnp.float32)
    basis = pl.pallas_call(
        main_kernel,
        out_shape=jax.ShapeDtypeStruct((BLOCKS * BACK, LANES), jnp.float32),
        in_specs=[whole],
        out_specs=whole,
        scratch_shapes=[pltpu.VMEM((LANES, LANES), jnp.float32)] + [flat] * 4 + [field] * 7,
        compiler_params=pltpu.CompilerParams(vmem_limit_bytes=40 * 2**20),
        name="basis",
    )(exchanged(packed, SEND))
    out = pl.pallas_call(
        final_kernel,
        out_shape=jax.ShapeDtypeStruct((8, columns), jnp.float32),
        in_specs=[whole],
        out_specs=held,
        scratch_shapes=[strip, pltpu.SemaphoreType.DMA((PARTS,))],
        compiler_params=pltpu.CompilerParams(vmem_limit_bytes=40 * 2**20),
        name="combine",
    )(exchanged(basis, BACK))
    return out.reshape(1, 8, columns)


def solution(mesh):
    return jax.shard_map(
        body,
        mesh=mesh,
        in_specs=(P("tm", "space", None), P("space", None)),
        out_specs=P("tm", "space", None),
        check_vma=False,
    )
```

```python
import jax
import jax.numpy as jnp
from jax import lax
from jax.experimental import pallas as pl
from jax.experimental.pallas import tpu as pltpu
from jax.sharding import PartitionSpec as P

STEPS = 8
STRIPS = 16
BLOCKS = STEPS * STRIPS
LANES = 128
HALO = 16
WIDE = LANES + 2 * HALO
PAD = 8
TALL = WIDE + 2 * PAD
TILES = WIDE // 8
SEND = 11
BACK = 25
CHUNKS = 1
PARTS = 2


def lane_of(shape):
    return lax.broadcasted_iota(jnp.int32, shape, 1)


def row_of(shape):
    return lax.broadcasted_iota(jnp.int32, shape, 0)


def pack_kernel(f_hbm, k_hbm, out_ref, f_ref, k_ref, side_ref, sems):
    step = lax.axis_index("tm").astype(jnp.int32)
    row = pltpu.make_async_copy(k_hbm.at[pl.ds(step, 1), :], k_ref, sems.at[CHUNKS])
    width = BLOCKS * LANES // CHUNKS

    def incoming(n):
        part = pl.ds(n * width, width)
        return pltpu.make_async_copy(f_hbm.at[:, part], f_ref.at[:, part], sems.at[n])

    def ready(n):
        return BLOCKS if n == CHUNKS - 1 else (n + 1) * BLOCKS // CHUNKS - 8

    row.start()
    for n in range(CHUNKS):
        incoming(n).start()

    lane = lane_of((8, LANES))
    zero = jnp.zeros((8, LANES), jnp.float32)

    def tile(ref, d):
        return ref[:, d * LANES : (d + 1) * LANES]

    def rolled(d):
        if d < 0 or d >= BLOCKS:
            return zero
        return pltpu.roll(tile(f_ref, d), 14, 1)

    def spread(d):
        if d < 0 or d >= BLOCKS:
            return zero
        return jnp.broadcast_to(tile(k_ref, d), (8, LANES))

    row.wait()
    before, here, done = rolled(-1), None, 0
    for n in range(CHUNKS):
        incoming(n).wait()
        here = rolled(0) if n == 0 else here
        for d in range(done, ready(n)):
            after = rolled(d + 1)
            beside = jnp.where(lane >= 64, spread(d - 1), spread(d + 1))
            beside = pltpu.roll(beside, 16, 1, stride=4, stride_axis=0)
            side_ref[8 * d : 8 * d + 8, :] = jnp.where(lane < 14, before, jnp.where(lane < 28, after, beside))
            out_ref[d * SEND : d * SEND + 8, :] = tile(f_ref, d)
            out_ref[d * SEND + 10 : d * SEND + 11, :] = tile(k_ref, d)
            before, here = here, after
        for d in range(done, ready(n), 4):
            group = [side_ref[pl.ds(8 * d + q, 8, stride=4), :] for q in range(4)]
            group = [group[0]] + [pltpu.roll(group[q], 32 * q, 1) for q in range(1, 4)]
            folded = jnp.where(lane < 64, jnp.where(lane < 32, *group[:2]), jnp.where(lane < 96, *group[2:]))
            for m in range(4):
                at = (d + m) * SEND + 8
                out_ref[at : at + 2, :] = folded[2 * m : 2 * m + 2]
        done = ready(n)


def main_kernel(in_ref, out_ref, sides, k, s, gn, gw, r0, r1, a, b, q0, q1, q2):
    lane = lane_of((8, LANES))
    sub = row_of((8, LANES))
    edge = jnp.zeros((PAD, LANES), jnp.float32)
    edges = jnp.zeros((STEPS, PAD, LANES), jnp.float32)
    for ref in (k, s, gn, gw):
        ref[0:PAD, :] = edge
        ref[PAD + WIDE : TALL, :] = edge
    for ref in (r0, r1, a, b, q0, q1, q2):
        ref[:, 0:PAD, :] = edges
        ref[:, PAD + WIDE : TALL, :] = edges

    for rows in (slice(PAD, PAD + 2), slice(PAD + WIDE - 2, PAD + WIDE)):
        r0[:, rows, :] = jnp.zeros((STEPS, 2, LANES), jnp.float32)
    own = slice(PAD + HALO, PAD + HALO + LANES)
    beside = []
    wide = lane_of((STRIPS, LANES))
    for low in range(0, STEPS, 4):
        for t in range(low, low + 4):
            base = SEND * STRIPS * t
            rows = [in_ref[base + SEND * i : base + SEND * i + 8, :] for i in range(STRIPS)]
            r0[t, own, :] = jnp.concatenate(rows, 0).T
        for j in range(2):
            packed = [in_ref[pl.ds(SEND * STRIPS * (low + m) + 8 + j, STRIPS, stride=SEND), :] for m in range(4)]
            for q in range(4):
                moved = [v if m == q else pltpu.roll(v, 32 * (m - q) % LANES, 1) for m, v in enumerate(packed)]
                joined = jnp.where(wide < 64, jnp.where(wide < 32, *moved[:2]), jnp.where(wide < 96, *moved[2:]))
                sides[pl.ds(4 * j + q, STRIPS, stride=8), :] = joined
        turned = sides[...].T
        for m in range(4):
            r0[low + m, PAD + 2 : PAD + HALO, :] = turned[32 * m : 32 * m + 14]
            r0[low + m, PAD + HALO + LANES : PAD + WIDE - 2, :] = turned[32 * m + 14 : 32 * m + 28]
            beside.append(turned[32 * m + 28 : 32 * m + 32])
    rows = [in_ref[pl.ds(SEND * i + 10, 8, stride=SEND * STRIPS), :] for i in range(STRIPS)]
    k[own, :] = jnp.concatenate(rows, 0).T
    for r in range(8):
        made = jnp.zeros((4, LANES), jnp.float32)
        for t in range(STEPS):
            moved = beside[t] if t == r else pltpu.roll(beside[t], (t - r) % LANES, 1)
            made = jnp.where(lane[:4] % 8 == t, moved, made)
        v = 4 * (7 - r)
        to = PAD + v if v < HALO else PAD + LANES + v
        k[to : to + 4, :] = made

    def at(i, offset=0):
        return pl.ds(pl.multiple_of(8 * i + PAD, 8) + offset, 8)

    def halves(i):
        mid = k[at(i), :]
        up = jnp.where(lane == 0, 0.0, pltpu.roll(mid, 1, 1))
        return mid, 0.5 * (mid + up), 0.5 * (mid + k[at(i, -1), :])

    @pl.loop(0, TILES, unroll=True)
    def _(i):
        mid, north, west = halves(i)
        down = jnp.where(lane == LANES - 1, 0.0, pltpu.roll(mid, LANES - 1, 1))
        south = 0.5 * (mid + down)
        east = 0.5 * (mid + k[at(i, 1), :])
        scale = 1.0 / jnp.sqrt(1.0 + north + south + west + east)
        s[at(i), :] = scale
        r0[:, at(i), :] = scale * r0[:, at(i), :]

    block = lax.axis_index("tm") * STRIPS + lax.axis_index("space")
    origin = block.astype(jnp.int32) * LANES - HALO

    @pl.loop(0, TILES, unroll=True)
    def _(i):
        _, north, west = halves(i)
        scale = s[at(i), :]
        column = origin + 8 * i + sub
        inside = (column > 0) & (column < BLOCKS * LANES)
        gn[at(i), :] = jnp.where(lane == 0, 0.0, north * scale * pltpu.roll(scale, 1, 1))
        gw[at(i), :] = jnp.where(inside, west * scale * s[at(i, -1), :], 0.0)

    def sweep(src, low, high, emit, count):
        def one(i, sums):
            north, west, east = gn[at(i), :], gw[at(i), :], gw[at(i, 1), :]
            x, left, right = src[:, at(i), :], src[:, at(i, -1), :], src[:, at(i, 1), :]
            g = north * pltpu.roll(x, 1, 2) + pltpu.roll(north * x, LANES - 1, 2)
            terms = emit(i, x, g + (west * left + east * right))
            own = (i >= HALO // 8) & (i < (HALO + LANES) // 8)
            return tuple(c + jnp.where(own, jnp.sum(v, axis=0), 0.0) for c, v in zip(sums, terms))

        zero = jnp.zeros((8, LANES), jnp.float32)
        return lax.fori_loop(low, high, one, (zero,) * count, unroll=True)

    def turned_in_time(x):
        return jnp.concatenate([x[t : t + 1] for t in reversed(range(STEPS))], 0)

    def polynomial(src, dst, bounds, emit, count):
        def start(i, x, g):
            a[:, at(i), :] = 0.5 * (g + x)
            return ()

        def middle(i, x, g):
            b[:, at(i), :] = g + 0.125 * src[:, at(i), :]
            return ()

        def end(i, x, g):
            given = src[:, at(i), :]
            made = g + 0.75 * given
            dst[:, at(i), :] = made
            return emit(i, given, made)

        sweep(src, *bounds[0], start, 0)
        sweep(a, *bounds[1], middle, 0)
        return sweep(b, *bounds[2], end, count)

    def operate(src, dst, bounds, later, emit, count):
        nothing = jnp.zeros((1, 8, LANES), jnp.float32)

        def act(i, x, g):
            inverse = s[at(i), :] * s[at(i), :]
            other = jnp.concatenate([x[1:], nothing] if later else [nothing, x[:-1]], 0)
            made = x - g - inverse * other
            dst[:, at(i), :] = made
            return emit(x, made)

        return sweep(src, *bounds, act, count)

    def same(i, v, q):
        return (v * q,)

    def mirrored(x, r):
        return (r * turned_in_time(x),)

    def send(field, ref, mirror):
        for t in range(STEPS):
            turned = (s[own, :] * ref[STEPS - 1 - t if mirror else t, own, :]).T
            for i in range(STRIPS):
                to = BACK * (STRIPS * t + i) + 8 * field
                out_ref[to : to + 8, :] = turned[8 * i : 8 * i + 8]

    full, most = (0, TILES), (1, TILES - 1)
    (m0,) = polynomial(r0, q0, (full, full, full), same, 1)
    send(0, q0, True)
    (m1,) = operate(q0, r1, full, True, mirrored, 1)
    (m2,) = polynomial(r1, q1, (full, most, most), same, 1)
    send(1, q1, False)
    operate(q1, r0, most, False, lambda x, r: (), 0)
    m4, m3 = polynomial(
        r0, q2, (most, most, most), lambda i, v, q: (v * q, r1[:, at(i), :] * turned_in_time(q)), 2
    )
    (m5,) = operate(q2, a, most, True, mirrored, 1)

    def square(i, x, g):
        b[:, at(i), :] = g
        return (x * (0.75 * x + 0.125 * g) + 0.5 * (g * g),)

    (m6,) = sweep(a, *most, square, 1)

    def edges_of(i, total):
        x = b[:, at(i), :]
        g = gn[at(i), :] * pltpu.roll(x, 1, 2) + gw[at(i), :] * b[:, at(i, -1), :]
        return total + jnp.sum(x * g, axis=0)

    m7 = lax.fori_loop(HALO // 8, (HALO + LANES) // 8, edges_of, jnp.zeros((8, LANES), jnp.float32), unroll=True)

    moments = jnp.zeros((8, LANES), jnp.float32)
    for n, value in enumerate((m0, m1, m2, m3, m4, m5, m6 + m7)):
        moments = jnp.where(sub == n, jnp.sum(value, axis=0, keepdims=True), moments)
    totals = jnp.sum(moments, axis=1, keepdims=True)
    line = jnp.sum(jnp.where(lane == sub, totals, 0.0), axis=0, keepdims=True)

    send(2, q2, True)
    for d in range(BLOCKS):
        out_ref[BACK * d + 24 : BACK * d + 25, :] = line


def coefficients(m):
    def combined(p, q, shift):
        total = None
        for i, x in enumerate(p):
            for j, y in enumerate(q):
                if x is not None and y is not None:
                    term = x * y * m[i + j + shift]
                    total = term if total is None else total + term
        return total

    def plus(*pairs):
        made = []
        for entries in zip(*[v for _, v in pairs]):
            total = None
            for (factor, _), e in zip(pairs, entries):
                if e is not None and factor is not None:
                    total = factor * e if total is None else total + factor * e
            made.append(total)
        return made

    one = jnp.ones_like(m[0])
    nil = jnp.zeros_like(m[0])
    none = [None] * 4
    vec, vec_old = [one, None, None, None], none
    gamma, gamma_old = jnp.sqrt(m[0]), one
    w, w_old, x = none, none, none
    c = c_old = one
    s = s_old = nil
    eta = gamma
    for _ in range(3):
        z = plus((1.0 / gamma, vec))
        image = [None] + z[:3]
        delta = combined(z, z, 1)
        new = plus((one, image), (-delta / gamma, vec), (-gamma / gamma_old, vec_old))
        gamma_new = jnp.sqrt(jnp.maximum(combined(new, new, 0), 0.0))
        a0 = c * delta - c_old * s * gamma
        a1 = jnp.sqrt(a0 * a0 + gamma_new * gamma_new)
        a2 = s * delta + c_old * c * gamma
        a3 = s_old * gamma
        c_new, s_new = a0 / a1, gamma_new / a1
        w_new = plus((1.0 / a1, z), (-a3 / a1, w_old), (-a2 / a1, w))
        x = plus((one, x), (c_new * eta, w_new))
        eta = -s_new * eta
        vec_old, vec, gamma_old, gamma = vec, new, gamma, gamma_new
        w_old, w, c_old, c, s_old, s = w, w_new, c, c_new, s, s_new
    return x[:3]


def final_kernel(in_ref, out_hbm, out_ref, sems):
    total = jnp.zeros((8, LANES), jnp.float32)
    for j in range(BLOCKS // 8):
        total = total + in_ref[pl.ds(24 + 8 * BACK * j, 8, stride=BACK), :]
    lane = lane_of((8, LANES))
    line = jnp.broadcast_to(jnp.sum(total, axis=0, keepdims=True), (8, LANES))
    m = [jnp.broadcast_to(jnp.sum(jnp.where(lane == n, line, 0.0), axis=1, keepdims=True), (8, LANES)) for n in range(7)]
    x0, x1, x2 = coefficients(m)
    width = BLOCKS // PARTS

    def outgoing(n):
        part = pl.ds(n * width * LANES, width * LANES)
        return pltpu.make_async_copy(out_ref.at[:, part], out_hbm.at[:, part], sems.at[n])

    for n in range(PARTS):
        for d in range(n * width, (n + 1) * width):
            at = BACK * d
            first, second, third = in_ref[at : at + 8, :], in_ref[at + 8 : at + 16, :], in_ref[at + 16 : at + 24, :]
            out_ref[:, d * LANES : (d + 1) * LANES] = x0 * first + x1 * second + x2 * third
        outgoing(n).start()
    for n in range(PARTS):
        outgoing(n).wait()


def exchanged(blocks, rows):
    pieces = blocks.reshape(-1).reshape(BLOCKS, rows, 1, LANES)
    moved = lax.all_to_all(pieces, ("tm", "space"), split_axis=0, concat_axis=0)
    return moved.reshape(-1).reshape(BLOCKS * rows, LANES)


def in_hbm(array):
    return pltpu.with_memory_space_constraint(array, pltpu.HBM)


def body(forcing, conductivity):
    columns = forcing.shape[2]
    whole, held = pl.BlockSpec(memory_space=pltpu.VMEM), pl.BlockSpec(memory_space=pl.ANY)
    strip = pltpu.VMEM((8, columns), jnp.float32)
    packed = pl.pallas_call(
        pack_kernel,
        out_shape=pltpu.VMEM((BLOCKS * SEND, LANES), jnp.float32),
        in_specs=[held, held],
        out_specs=whole,
        scratch_shapes=[
            strip,
            pltpu.VMEM((1, columns), jnp.float32),
            pltpu.VMEM((BLOCKS * 8, LANES), jnp.float32),
            pltpu.SemaphoreType.DMA((CHUNKS + 1,)),
        ],
        compiler_params=pltpu.CompilerParams(vmem_limit_bytes=40 * 2**20),
        name="pack",
    )(in_hbm(forcing.reshape(8, columns)), in_hbm(conductivity))
    flat, field = pltpu.VMEM((TALL, LANES), jnp.float32), pltpu.VMEM((STEPS, TALL, LANES), jnp.float32)
    basis = pl.pallas_call(
        main_kernel,
        out_shape=jax.ShapeDtypeStruct((BLOCKS * BACK, LANES), jnp.float32),
        in_specs=[whole],
        out_specs=whole,
        scratch_shapes=[pltpu.VMEM((LANES, LANES), jnp.float32)] + [flat] * 4 + [field] * 7,
        compiler_params=pltpu.CompilerParams(vmem_limit_bytes=40 * 2**20),
        name="basis",
    )(exchanged(packed, SEND))
    out = pl.pallas_call(
        final_kernel,
        out_shape=jax.ShapeDtypeStruct((8, columns), jnp.float32),
        in_specs=[whole],
        out_specs=held,
        scratch_shapes=[strip, pltpu.SemaphoreType.DMA((PARTS,))],
        compiler_params=pltpu.CompilerParams(vmem_limit_bytes=40 * 2**20),
        name="combine",
    )(exchanged(basis, BACK))
    return out.reshape(1, 8, columns)


def solution(mesh):
    return jax.shard_map(
        body,
        mesh=mesh,
        in_specs=(P("tm", "space", None), P("space", None)),
        out_specs=P("tm", "space", None),
        check_vma=False,
    )
```
